256 devices in a mesh: seq: 64 (over z, x_lo, y), tp: 4 (over x_hi, core).
Axes of the slice: x: 4 (x_hi: 2, x_lo: 2; x = x_hi * 2 + x_lo), y: 4, z: 8, core: 2. Of those that a mesh axis runs over, the one named last changes fastest.
Arguments:
- queries: bfloat16 [2, 4096, 4096], P(None, 'seq', 'tp'), may hold values from -8 to 8
- key_projected: bfloat16 [2, 4096, 512], P(None, 'seq', 'tp'), may hold values from -4 to 4
- values: bfloat16 [2, 4096, 512], P(None, 'seq', 'tp'), may hold values from -6 to 6
- segments: int32 [2, 4096], replicated, may hold values from 0 to 3, never falling along the last dimension, each value on 1 to 2048 neighbouring positions
- out_weight: bfloat16 [4096, 4096], P('tp'), may hold values from -0.09375 to 0.09375
Outputs:
- projected: bfloat16 [2, 4096, 4096], P(None, 'seq')
The draws below stay inside these ranges and needn't reach their ends.
Inputs may be any that keep to these rules, and one draw needn't show every extreme that they name: `segments`: along each sequence the numbers never fall; a segment spans 1 to 2048 positions and one spans exactly 2048.
All inputs are finite; a program needn't handle non-finite values.
Results may differ from the reference program's by a relative error of at most 0.0058.
Values may be sent and summed in bfloat16 or wider, within the bound.
No kernel may reach another device: no remote copies, remote signals or barrier semaphores. Data moves between devices by JAX's collectives and lax.ppermute only.
A program may use at most 64 MiB of HBM per device.

```python
import math
import jax
import jax.numpy as jnp
import numpy as np
from jax import lax

QUERY_HEAD_COUNT = 32
KEY_VALUE_HEADS = 4
HEAD_DIMENSION = 128
DW = 4096
SEQUENCE_COUNT = 2
SEGS = 4
SEQUENCE_LENGTH = 4096
SEG_MOST = 2048


def draw_queries(key, part):
    key = jax.random.fold_in(key, 11)
    field_name = jnp.clip(2.7 * jax.random.normal(key, (SEQUENCE_COUNT, SEQUENCE_LENGTH, QUERY_HEAD_COUNT, HEAD_DIMENSION), jnp.float32), -8.0, 8.0)
    return field_name.reshape(SEQUENCE_COUNT, SEQUENCE_LENGTH, QUERY_HEAD_COUNT * HEAD_DIMENSION).astype(jnp.bfloat16)


def draw_key_projected(key, part):
    key = jax.random.fold_in(key, 23)
    field_name = jnp.clip(jax.random.normal(key, (SEQUENCE_COUNT, SEQUENCE_LENGTH, KEY_VALUE_HEADS, HEAD_DIMENSION), jnp.float32), -4.0, 4.0)
    return field_name.reshape(SEQUENCE_COUNT, SEQUENCE_LENGTH, KEY_VALUE_HEADS * HEAD_DIMENSION).astype(jnp.bfloat16)


def block_scale(stream_key, dims, cuts, low, largest):
    factor_of = 1.0
    for axis_at, shards_of in cuts:
        steps = jax.random.uniform(jax.random.fold_in(jax.random.fold_in(stream_key, 6), axis_at), (shards_of,), jnp.float32, low / len(cuts), largest / len(cuts))
        factor_of = factor_of * jnp.repeat(jnp.exp(steps), dims[axis_at] // shards_of).reshape((-1,) + (1,) * (len(dims) - 1 - axis_at))
    return factor_of


def length_profile(number_of, total, most, lean):
    weights = [(1 << 20) // math.isqrt(rank ** lean) + 1 for rank in range(2, number_of + 1)]
    surplus, given = total - most - (number_of - 1), [1] * (number_of - 1)
    while surplus > 0:
        candidates = [i for i in range(number_of - 1) if given[i] < most]
        whole, budget = sum([weights[i] for i in candidates]), surplus
        for i in candidates:
            more = min(most - given[i], max(1, budget * weights[i] // whole), surplus)
            given[i] = given[i] + more
            surplus = surplus - more
    return np.array([most] + given)


def ragged_sizes(rng, amount, total, limit, skew):
    if amount == 2:
        one = jax.random.randint(rng, (), max(1, total - limit), min(limit, total - 1) + 1)
        return jnp.stack([one, total - one])
    tallies = jnp.asarray(length_profile(amount, total, limit, skew), jnp.int32)
    twos = (amount - 1) // 2
    giver, sink = tallies[1:1 + 2 * twos:2], tallies[2:2 + 2 * twos:2]
    room = jnp.minimum(giver - 1, limit - sink)
    shifted = jax.random.randint(jax.random.fold_in(rng, 1), (twos,), 0, 1 << 20) % (room + 1)
    tallies = tallies.at[1:1 + 2 * twos:2].set(giver - shifted).at[2:2 + 2 * twos:2].set(sink + shifted)
    return tallies[jax.random.permutation(jax.random.fold_in(rng, 2), amount)]


def bell_draw(key, extent, scale, most, cuts=(), kind=jnp.bfloat16):
    values = jax.random.normal(key, extent, jnp.float32) * scale
    if len(cuts) > 0:
        values = block_scale(key, extent, cuts, -0.22, 0.18) * values
    return jnp.clip(values, min=-most, max=most).astype(kind)


def setup_inputs(seed: int = 0) -> dict:
    seeds = jax.random.split(jax.random.key(seed), 6)
    return {
        "queries": draw_queries(jax.random.fold_in(seeds[5], 71), 0),
        "key_projected": draw_key_projected(jax.random.fold_in(seeds[5], 71), 0),
        "values": bell_draw(seeds[2], (SEQUENCE_COUNT, SEQUENCE_LENGTH, KEY_VALUE_HEADS * HEAD_DIMENSION), 1.0, 6.0, ((1, 64), (2, 4))),
        "segments": jax.vmap(lambda own: jnp.searchsorted(jnp.cumsum(ragged_sizes(own, SEGS, SEQUENCE_LENGTH, SEG_MOST, 0)), jnp.arange(SEQUENCE_LENGTH), side="right"))(jax.random.split(seeds[3], SEQUENCE_COUNT)).reshape((SEQUENCE_COUNT, SEQUENCE_LENGTH)).astype(jnp.int32),
        "out_weight": bell_draw(seeds[4], (QUERY_HEAD_COUNT * HEAD_DIMENSION, DW), (QUERY_HEAD_COUNT * HEAD_DIMENSION) ** -0.5, 0.09375, ((0, 4),)),
    }


def head_context(head_rows, key_rows, value_rows, seg_ids, factor):
    query_size = min(512, SEQUENCE_LENGTH)
    key_pos = jnp.arange(SEQUENCE_LENGTH, dtype=jnp.int32)
    starts = jnp.arange(SEQUENCE_LENGTH // query_size, dtype=jnp.int32) * query_size

    def per_block(pieces):
        query_block, offset = pieces
        query_pos = offset + jnp.arange(query_size, dtype=jnp.int32)
        query_seg = lax.dynamic_slice_in_dim(seg_ids, offset, query_size)
        logits = jnp.dot(query_block, key_rows.T, preferred_element_type=jnp.float32) * factor
        allowed = (key_pos[None, :] <= query_pos[:, None]) & (seg_ids[None, :] == query_seg[:, None])
        masked = jnp.where(allowed, logits, -1e+30)
        row_top = lax.optimization_barrier(jnp.max(masked, axis=1, keepdims=True))
        kept_exp = jnp.where(allowed, jnp.exp(masked - row_top), 0.0)
        row_sum = lax.optimization_barrier(jnp.sum(kept_exp, axis=1, keepdims=True))
        weights = (kept_exp / row_sum).astype(jnp.bfloat16)
        return jnp.dot(weights, value_rows, preferred_element_type=jnp.float32).astype(jnp.bfloat16)
    blocks = lax.map(per_block, (head_rows.reshape(SEQUENCE_LENGTH // query_size, query_size, HEAD_DIMENSION), starts))
    return blocks.reshape(SEQUENCE_LENGTH, HEAD_DIMENSION)

def reference(queries, key_projected, values, segments, out_weight):
    head_group = QUERY_HEAD_COUNT // KEY_VALUE_HEADS
    factor = 1.0 / math.sqrt(HEAD_DIMENSION)
    owners = jnp.arange(QUERY_HEAD_COUNT, dtype=jnp.int32) // head_group
    outputs = []
    for batch_number in range(SEQUENCE_COUNT):
        query_split = queries[batch_number].reshape(SEQUENCE_LENGTH, QUERY_HEAD_COUNT, HEAD_DIMENSION).transpose(1, 0, 2)
        key_divided = key_projected[batch_number].reshape(SEQUENCE_LENGTH, KEY_VALUE_HEADS, HEAD_DIMENSION).transpose(1, 0, 2)
        value_divided = values[batch_number].reshape(SEQUENCE_LENGTH, KEY_VALUE_HEADS, HEAD_DIMENSION).transpose(1, 0, 2)
        seg_row = segments[batch_number]

        def per_head(pieces):
            head_rows, owner = pieces
            return head_context(head_rows, key_divided[owner], value_divided[owner], seg_row, factor)
        context = lax.map(per_head, (query_split, owners))
        context = context.transpose(1, 0, 2).reshape(SEQUENCE_LENGTH, QUERY_HEAD_COUNT * HEAD_DIMENSION)
        outputs.append(jnp.dot(context, out_weight, preferred_element_type=jnp.float32).astype(jnp.bfloat16))
    return jnp.stack(outputs)
```

```python
import functools
import math

import jax
import jax.numpy as jnp
from jax import lax
from jax.experimental import pallas as pl
from jax.experimental.pallas import tpu as pltpu
from jax.sharding import PartitionSpec as P

NZ, NX, NY, NH, NC = 8, 2, 4, 2, 2
AXES = ("seq", "tp")
MASKED = -1e30
NEAR, FAR = (0, 1), (2, 3, 4)


def shift(array, move):
    pairs = []
    for z in range(NZ):
        for x in range(NX):
            for y in range(NY):
                for h in range(NH):
                    for c in range(NC):
                        to = move(z, x, y, h, c)
                        if to is not None:
                            flat = lambda a, b, d, e, f: (((a * NX + b) * NY + d) * NH + e) * NC + f
                            pairs.append((flat(z, x, y, h, c), flat(*to)))
    return lax.ppermute(array, AXES, pairs)


def swap_x(array):
    return shift(array, lambda z, x, y, h, c: (z, 1 - x, y, h, c))


def swap_core(array):
    return shift(array, lambda z, x, y, h, c: (z, x, y, h, 1 - c))


def swap_high(array):
    return shift(array, lambda z, x, y, h, c: (z, x, y, 1 - h, c))


def swap_both(array):
    return shift(array, lambda z, x, y, h, c: (z, 1 - x, y, 1 - h, c))


def shift_z(array, by):
    return shift(array, lambda z, x, y, h, c: (z + by, x, y, h, c) if z + by < NZ else None)


def shift_y(array, by):
    return shift(array, lambda z, x, y, h, c: (z, x, (y + by) % NY, h, c))


def row_limits(info, rows, block):
    z, x, y = info[0], info[1], info[2]
    row = lax.broadcasted_iota(jnp.int32, (rows, 1), 0)
    layer = block * NX * NY
    own = z * layer + x * (block * NY) + y * block
    other = z * layer + (1 - x) * (block * NY) + y * block
    last = jnp.where(row < block, own + row, other + row - block)
    first = jnp.zeros_like(last)
    for at in range(4):
        start = info[4 + at]
        first = jnp.where(start <= last, jnp.maximum(first, start), first)
    return first, last


def key_positions(info, layer_back, column, rows, block):
    z, x = info[0], info[1]
    lane = lax.broadcasted_iota(jnp.int32, (1, rows), 1)
    layer = block * NX * NY
    base = (z - layer_back) * layer + column * block
    own, other = base + x * (block * NY), base + (1 - x) * (block * NY)
    return jnp.where(lane < block, own + lane, other + lane - block)


def bias_of(info, first, last, layers, rows, block):
    parts = []
    for back in (0, 1, 3, 2):
        column = lax.rem(info[2] + NY - back, NY)
        tiles = []
        for layer_back in layers:
            at = key_positions(info, layer_back, column, rows, block)
            tiles.append(jnp.where((at >= first) & (at <= last), 0.0, MASKED))
        parts.append(jnp.concatenate(tiles, axis=1))
    return parts


def attend_tiles(query, kv_refs, bias, top, scale):
    scores = []
    for ref, part in zip(kv_refs, bias):
        keys = ref[0].reshape(-1, query.shape[1])
        raw = lax.dot_general(query, keys, (((1,), (1,)), ((), ())), preferred_element_type=jnp.float32)
        scores.append(raw + part)
    highest = functools.reduce(jnp.maximum, [jnp.max(s, axis=1, keepdims=True) for s in scores])
    if top is not None:
        highest = jnp.maximum(highest, top)
    total, mixed = 0.0, 0.0
    for ref, s in zip(kv_refs, scores):
        kept = jnp.exp2((s - highest) * scale)
        total = total + jnp.sum(kept, axis=1, keepdims=True)
        rows = ref[1].reshape(-1, query.shape[1])
        mixed = mixed + jnp.dot(kept.astype(jnp.bfloat16), rows, preferred_element_type=jnp.float32)
    return highest, total, mixed


def head_query(own_ref, other_ref, head, size):
    at = slice(head * size, (head + 1) * size)
    return jnp.concatenate([own_ref[:, at], other_ref[:, at]], axis=0)


def near_kernel(heads, size, block, info, own_ref, other_ref, k0, k1, k2, k3, mixed_ref, stat_ref):
    scale = math.log2(math.e) / math.sqrt(size)
    rows = 2 * block
    first, last = row_limits(info, rows, block)
    bias = bias_of(info, first, last, NEAR, rows, block)
    lane = lax.broadcasted_iota(jnp.int32, (rows, 128), 1)
    stats = jnp.zeros((rows, 128), jnp.float32)
    for head in range(heads):
        query = head_query(own_ref, other_ref, head, size)
        highest, total, mixed = attend_tiles(query, (k0, k1, k2, k3), bias, None, scale)
        mixed_ref[:, head * size:(head + 1) * size] = mixed
        stats = jnp.where(lane == head, highest, stats)
        stats = jnp.where(lane == heads + head, total, stats)
    stat_ref[...] = stats


def far_kernel(heads, size, block, info, own_ref, other_ref, k0, k1, k2, k3, mixed_ref, stat_ref, weight_hbm,
               keep_ref, give_ref, weight, context, sem):
    copy = pltpu.make_async_copy(weight_hbm, weight, sem)
    copy.start()
    scale = math.log2(math.e) / math.sqrt(size)
    rows = 2 * block
    first, last = row_limits(info, rows, block)
    bias = bias_of(info, first, last, FAR, rows, block)
    stats = stat_ref[...]
    for head in range(heads):
        at = slice(head * size, (head + 1) * size)
        query = head_query(own_ref, other_ref, head, size)
        old_top, old_total = stats[:, head:head + 1], stats[:, heads + head:heads + head + 1]
        highest, total, mixed = attend_tiles(query, (k0, k1, k2, k3), bias, old_top, scale)
        fade = jnp.exp2((old_top - highest) * scale)
        mixed = mixed + mixed_ref[:, at] * fade
        total = total + old_total * fade
        context[:, at] = (mixed / total).astype(jnp.bfloat16)
    copy.wait()
    half = keep_ref.shape[1]
    core = info[3]
    mine = pl.ds(pl.multiple_of(core * half, 128), half)
    theirs = pl.ds(pl.multiple_of((1 - core) * half, 128), half)
    give_ref[...] = jnp.dot(context[...], weight[:, theirs], preferred_element_type=jnp.float32).astype(jnp.bfloat16)
    keep_ref[...] = jnp.dot(context[...], weight[:, mine], preferred_element_type=jnp.float32)


def body(queries, key_projected, values, segments, out_weight):
    _, block, width = queries.shape
    size = key_projected.shape[2]
    heads = width // size
    features = out_weight.shape[1]
    rows = 2 * block
    seq, tp = lax.axis_index("seq"), lax.axis_index("tp")
    z, x, y = seq // (NX * NY), (seq // NY) % NX, seq % NY
    high, core = tp // NC, tp % NC
    batch = x ^ high

    pair = jnp.stack([key_projected, values], axis=1)
    pick = lambda a, i: lax.dynamic_index_in_dim(a, i, 0, keepdims=False)
    unit = jnp.concatenate([pick(pair, batch), swap_x(pick(pair, 1 - batch))], axis=1)
    own_q = pick(queries, batch)
    other_q = swap_x(pick(queries, 1 - batch))

    seg = pick(segments, batch)
    starts = jnp.sum((seg[None, :] < jnp.arange(4, dtype=jnp.int32)[:, None]).astype(jnp.int32), axis=1)
    info = jnp.concatenate([jnp.stack([z, x, y, core]).astype(jnp.int32), starts])

    near = jnp.stack([unit, shift_z(unit, 1)], axis=1)
    near_all = [near] + [shift_y(near, by) for by in (1, 3, 2)]
    far = jnp.concatenate([shift_z(near, 2), shift_z(unit, 4)[:, None]], axis=1)
    far_all = [far] + [shift_y(far, by) for by in (1, 3, 2)]

    smem = pl.BlockSpec(memory_space=pltpu.SMEM)
    vmem = pl.BlockSpec(memory_space=pltpu.VMEM)
    mixed, stats = pl.pallas_call(
        functools.partial(near_kernel, heads, size, block),
        out_shape=(
            jax.ShapeDtypeStruct((rows, width), jnp.float32),
            jax.ShapeDtypeStruct((rows, 128), jnp.float32),
        ),
        in_specs=[smem] + [vmem] * 6,
        out_specs=(vmem, vmem),
        compiler_params=pltpu.CompilerParams(vmem_limit_bytes=32 * 1024 * 1024),
        cost_estimate=pl.CostEstimate(flops=4 * rows * width * 8 * rows, bytes_accessed=2 << 20, transcendentals=heads * rows * 8 * rows),
    )(info, own_q, other_q, *near_all)
    keep, give = pl.pallas_call(
        functools.partial(far_kernel, heads, size, block),
        out_shape=(
            jax.ShapeDtypeStruct((rows, features // 2), jnp.float32),
            jax.ShapeDtypeStruct((rows, features // 2), jnp.bfloat16),
        ),
        in_specs=[smem] + [vmem] * 8 + [pl.BlockSpec(memory_space=pl.ANY)],
        out_specs=(vmem, vmem),
        scratch_shapes=[
            pltpu.VMEM(out_weight.shape, jnp.bfloat16),
            pltpu.VMEM((rows, width), jnp.bfloat16),
            pltpu.SemaphoreType.DMA,
        ],
        compiler_params=pltpu.CompilerParams(vmem_limit_bytes=40 * 1024 * 1024),
    )(info, own_q, other_q, *far_all, mixed, stats, out_weight)

    summed = keep + swap_core(give).astype(jnp.float32)
    final = (summed[:block] + swap_both(summed[block:].astype(jnp.bfloat16)).astype(jnp.float32)).astype(jnp.bfloat16)
    other = swap_high(final)
    final_far, other_far = swap_core(final), swap_core(other)
    left = jnp.where(core == 0, jnp.stack([final, other]), jnp.stack([final_far, other_far]))
    right = jnp.where(core == 0, jnp.stack([final_far, other_far]), jnp.stack([final, other]))
    whole = jnp.concatenate([left, right], axis=2)
    return jnp.where(batch == 0, whole, whole[::-1])


def solution(mesh):
    in_specs = (
        P(None, "seq", "tp"),
        P(None, "seq", "tp"),
        P(None, "seq", "tp"),
        P(),
        P("tp", None),
    )
    return jax.shard_map(body, mesh=mesh, in_specs=in_specs, out_specs=P(None, "seq", None), check_vma=False)
```

```python
import functools
import math

import jax
import jax.numpy as jnp
from jax import lax
from jax.experimental import pallas as pl
from jax.experimental.pallas import tpu as pltpu
from jax.sharding import PartitionSpec as P

NZ, NX, NY, NH, NC = 8, 2, 4, 2, 2
AXES = ("seq", "tp")
MASKED = -1e30
NEAR, FAR = (0, 1), (2, 3, 4)
GROUP = 2


def shift(array, move):
    pairs = []
    for z in range(NZ):
        for x in range(NX):
            for y in range(NY):
                for h in range(NH):
                    for c in range(NC):
                        flat = lambda a, b, d, e, f: (((a * NX + b) * NY + d) * NH + e) * NC + f
                        pairs.append((flat(z, x, y, h, c), flat(*move(z, x, y, h, c))))
    return lax.ppermute(array, AXES, pairs)


def swap_x(array):
    return shift(array, lambda z, x, y, h, c: (z, 1 - x, y, h, c))


def swap_core(array):
    return shift(array, lambda z, x, y, h, c: (z, x, y, h, 1 - c))


def swap_high(array):
    return shift(array, lambda z, x, y, h, c: (z, x, y, 1 - h, c))


def swap_both(array):
    return shift(array, lambda z, x, y, h, c: (z, 1 - x, y, 1 - h, c))


def shift_z(array, by):
    return shift(array, lambda z, x, y, h, c: ((z + by) % NZ, x, y, h, c))


def shift_y(array, by):
    return shift(array, lambda z, x, y, h, c: (z, x, (y + by) % NY, h, c))


def row_limits(info, rows, block):
    z, x, y = info[0], info[1], info[2]
    row = lax.broadcasted_iota(jnp.int32, (rows, 1), 0)
    layer = block * NX * NY
    own = z * layer + x * (block * NY) + y * block
    other = z * layer + (1 - x) * (block * NY) + y * block
    last = jnp.where(row < block, own + row, other + row - block)
    first = jnp.zeros_like(last)
    for at in range(4):
        start = info[4 + at]
        first = jnp.where(start <= last, jnp.maximum(first, start), first)
    return first, last


def key_positions(info, layer_back, column, rows, block):
    z, x = info[0], info[1]
    lane = lax.broadcasted_iota(jnp.int32, (1, rows), 1)
    layer = block * NX * NY
    base = (z - layer_back) * layer + column * block
    own, other = base + x * (block * NY), base + (1 - x) * (block * NY)
    return jnp.where(lane < block, own + lane, other + lane - block)


def bias_of(info, first, last, layers, rows, block):
    parts = []
    for back in (0, 1, 3, 2):
        column = lax.rem(info[2] + NY - back, NY)
        tiles = []
        for layer_back in layers:
            at = key_positions(info, layer_back, column, rows, block)
            tiles.append(jnp.where((at >= first) & (at <= last), 0.0, MASKED))
        parts.append(jnp.concatenate(tiles, axis=1))
    return parts


def attend_group(queries, kv_refs, bias, top, scale, heads):
    size = queries.shape[1]
    scores = []
    for ref, part in zip(kv_refs, bias):
        keys = ref[0].reshape(-1, size)
        raw = lax.dot_general(queries, keys, (((1,), (1,)), ((), ())), preferred_element_type=jnp.float32)
        scores.append((raw.reshape(heads, -1, raw.shape[1]) + part[None]).reshape(raw.shape))
    highest = functools.reduce(jnp.maximum, [jnp.max(s, axis=1, keepdims=True) for s in scores])
    if top is not None:
        highest = jnp.maximum(highest, top)
    offset = highest * scale
    total, mixed = 0.0, 0.0
    for ref, s in zip(kv_refs, scores):
        kept = jnp.exp2(s * scale - offset)
        total = total + jnp.sum(kept, axis=1, keepdims=True)
        mixed = mixed + jnp.dot(kept.astype(jnp.bfloat16), ref[1].reshape(-1, size), preferred_element_type=jnp.float32)
    return highest, total, mixed


def group_queries(own_ref, other_ref, heads, size):
    return jnp.concatenate([ref[:, h * size:(h + 1) * size] for h in heads for ref in (own_ref, other_ref)], axis=0)


def load_columns(info, own_half, weight_hbm, weight_ref, sem):
    half = weight_ref.shape[1]
    which = info[3] if own_half else 1 - info[3]
    return pltpu.make_async_copy(weight_hbm.at[:, pl.ds(pl.multiple_of(which * half, half), half)], weight_ref, sem)


def near_kernel(heads, size, block, info, own_ref, other_ref, k0, k1, k2, k3, weight_hbm, mixed_ref, stat_ref, weight_ref, sem):
    copy = load_columns(info, False, weight_hbm, weight_ref, sem)
    copy.start()
    scale = math.log2(math.e) / math.sqrt(size)
    rows = 2 * block
    first, last = row_limits(info, rows, block)
    bias = bias_of(info, first, last, NEAR, rows, block)
    lane = lax.broadcasted_iota(jnp.int32, (rows, 128), 1)
    stats = jnp.zeros((rows, 128), jnp.float32)
    for start in range(0, heads, GROUP):
        group = range(start, start + GROUP)
        queries = group_queries(own_ref, other_ref, group, size)
        highest, total, mixed = attend_group(queries, (k0, k1, k2, k3), bias, None, scale, GROUP)
        for i, head in enumerate(group):
            part = slice(i * rows, (i + 1) * rows)
            mixed_ref[:, head * size:(head + 1) * size] = mixed[part]
            stats = jnp.where(lane == head, highest[part], stats)
            stats = jnp.where(lane == heads + head, total[part], stats)
    stat_ref[...] = stats
    copy.wait()


def far_kernel(heads, size, block, info, own_ref, other_ref, k0, k1, k2, k3, mixed_ref, stat_ref, weight_hbm, context_ref, weight_ref, sem):
    copy = load_columns(info, True, weight_hbm, weight_ref, sem)
    copy.start()
    scale = math.log2(math.e) / math.sqrt(size)
    rows = 2 * block
    first, last = row_limits(info, rows, block)
    bias = bias_of(info, first, last, FAR, rows, block)
    stats = stat_ref[...]
    for start in range(0, heads, GROUP):
        group = range(start, start + GROUP)
        queries = group_queries(own_ref, other_ref, group, size)
        old_top = jnp.concatenate([stats[:, h:h + 1] for h in group], axis=0)
        highest, total, mixed = attend_group(queries, (k0, k1, k2, k3), bias, old_top, scale, GROUP)
        fade = jnp.exp2((old_top - highest) * scale)
        for i, head in enumerate(group):
            part, at = slice(i * rows, (i + 1) * rows), slice(head * size, (head + 1) * size)
            whole = total[part] + stats[:, heads + head:heads + head + 1] * fade[part]
            context_ref[:, at] = ((mixed[part] + mixed_ref[:, at] * fade[part]) / whole).astype(jnp.bfloat16)
    copy.wait()


def project_kernel(context_ref, weight_ref, out_ref):
    out_ref[...] = jnp.dot(context_ref[...], weight_ref[...], preferred_element_type=jnp.float32).astype(out_ref.dtype)


def body(queries, key_projected, values, segments, out_weight):
    _, block, width = queries.shape
    size = key_projected.shape[2]
    heads = width // size
    features = out_weight.shape[1]
    rows = 2 * block
    seq, tp = lax.axis_index("seq"), lax.axis_index("tp")
    z, x, y = seq // (NX * NY), (seq // NY) % NX, seq % NY
    high, core = tp // NC, tp % NC
    batch = x ^ high
    pick = lambda a, i, axis: lax.dynamic_index_in_dim(a, i, axis, keepdims=False)

    pair = jnp.stack([key_projected, values], axis=1)
    unit = jnp.concatenate([pick(pair, batch, 0), swap_x(pick(pair, 1 - batch, 0))], axis=1)
    near = jnp.stack([unit, shift_z(unit, 1)], axis=1)
    far = jnp.stack([shift_z(unit, by) for by in (2, 3, 4)], axis=1)
    near_all = [near] + [shift_y(near, by) for by in (1, 3, 2)]
    far_all = [far] + [shift_y(far, by) for by in (1, 3, 2)]
    own_q = pick(queries, batch, 0)
    other_q = swap_x(pick(queries, 1 - batch, 0))

    seg = pick(segments, batch, 0)
    starts = jnp.sum((seg[None, :] < jnp.arange(4, dtype=jnp.int32)[:, None]).astype(jnp.int32), axis=1)
    info = jnp.concatenate([jnp.stack([z, x, y, core]).astype(jnp.int32), starts])

    smem = pl.BlockSpec(memory_space=pltpu.SMEM)
    vmem = pl.BlockSpec(memory_space=pltpu.VMEM)
    hbm = pl.BlockSpec(memory_space=pltpu.HBM)
    limit = pltpu.CompilerParams(vmem_limit_bytes=24 * 1024 * 1024)
    mixed, stats, weight_given = pl.pallas_call(
        functools.partial(near_kernel, heads, size, block),
        out_shape=(
            jax.ShapeDtypeStruct((rows, width), jnp.float32),
            jax.ShapeDtypeStruct((rows, 128), jnp.float32),
            jax.ShapeDtypeStruct((width, features // 2), jnp.bfloat16),
        ),
        in_specs=[smem] + [vmem] * 6 + [hbm],
        out_specs=(vmem, vmem, vmem),
        scratch_shapes=[pltpu.SemaphoreType.DMA],
        compiler_params=limit,
    )(info, own_q, other_q, *near_all, out_weight)
    context, weight_kept = pl.pallas_call(
        functools.partial(far_kernel, heads, size, block),
        out_shape=(
            jax.ShapeDtypeStruct((rows, width), jnp.bfloat16),
            jax.ShapeDtypeStruct((width, features // 2), jnp.bfloat16),
        ),
        in_specs=[smem] + [vmem] * 8 + [hbm],
        out_specs=(vmem, vmem),
        scratch_shapes=[pltpu.SemaphoreType.DMA],
        compiler_params=limit,
    )(info, own_q, other_q, *far_all, mixed, stats, out_weight)

    def project(weight, dtype):
        return pl.pallas_call(
            project_kernel,
            out_shape=jax.ShapeDtypeStruct((rows, features // 2), dtype),
            in_specs=[vmem, vmem],
            out_specs=vmem,
            compiler_params=limit,
        )(context, weight)

    given = swap_core(project(weight_given, jnp.bfloat16))
    summed = project(weight_kept, jnp.float32) + given.astype(jnp.float32)
    final = (summed[:block] + swap_both(summed[block:].astype(jnp.bfloat16)).astype(jnp.float32)).astype(jnp.bfloat16)
    other = swap_high(final)
    final_far, other_far = swap_core(final), swap_core(other)
    left = jnp.where(core == 0, jnp.stack([final, other]), jnp.stack([final_far, other_far]))
    right = jnp.where(core == 0, jnp.stack([final_far, other_far]), jnp.stack([final, other]))
    whole = jnp.concatenate([left, right], axis=2)
    return jnp.where(batch == 0, whole, whole[::-1])


def solution(mesh):
    in_specs = (
        P(None, "seq", "tp"),
        P(None, "seq", "tp"),
        P(None, "seq", "tp"),
        P(),
        P("tp", None),
    )
    return jax.shard_map(body, mesh=mesh, in_specs=in_specs, out_specs=P(None, "seq", None), check_vma=False)
```

```python
import functools
import math

import jax
import jax.numpy as jnp
from jax import lax
from jax.experimental import pallas as pl
from jax.experimental.pallas import tpu as pltpu
from jax.sharding import PartitionSpec as P

NZ, NX, NY, NH, NC = 8, 2, 4, 2, 2
AXES = ("seq", "tp")
MASKED = -1e30
NEAR, FAR = (0, 1, 2), (3, 4)
COLUMNS_BACK = (0, 1, 3, 2)
GROUP = 4
PIECES = 1
LONG = pl.CostEstimate(flops=4 << 30, bytes_accessed=16 << 20, transcendentals=4 << 20)
LIMIT = pltpu.CompilerParams(vmem_limit_bytes=24 * 1024 * 1024)
SMEM = pl.BlockSpec(memory_space=pltpu.SMEM)
VMEM = pl.BlockSpec(memory_space=pltpu.VMEM)
HBM = pl.BlockSpec(memory_space=pl.ANY)


def shift(array, move):
    flat = lambda z, x, y, h, c: (((z * NX + x) * NY + y) * NH + h) * NC + c
    devices = [
        (z, x, y, h, c)
        for z in range(NZ) for x in range(NX) for y in range(NY) for h in range(NH) for c in range(NC)
    ]
    return lax.ppermute(array, AXES, [(flat(*d), flat(*move(*d))) for d in devices])


def swap_x(array):
    return shift(array, lambda z, x, y, h, c: (z, 1 - x, y, h, c))


def swap_core(array):
    return shift(array, lambda z, x, y, h, c: (z, x, y, h, 1 - c))


def swap_high(array):
    return shift(array, lambda z, x, y, h, c: (z, x, y, 1 - h, c))


def swap_both(array):
    return shift(array, lambda z, x, y, h, c: (z, 1 - x, y, 1 - h, c))


def shift_z(array, by):
    return shift(array, lambda z, x, y, h, c: ((z + by) % NZ, x, y, h, c))


def shift_y(array, by):
    return shift(array, lambda z, x, y, h, c: (z, x, (y + by) % NY, h, c))


def row_limits(info, which, block):
    z, x, y = info[0], info[1], info[2]
    base = (z * NX + (1 - x if which else x)) * (NY * block) + y * block
    last = base + lax.broadcasted_iota(jnp.int32, (block, 1), 0)
    first = jnp.zeros_like(last)
    for at in range(4):
        start = info[4 + at]
        first = jnp.where(start <= last, jnp.maximum(first, start), first)
    return first, last


def bias_of(info, which, layers, block):
    z, x, y = info[0], info[1], info[2]
    first, last = row_limits(info, which, block)
    lane = lax.broadcasted_iota(jnp.int32, (1, 2 * block), 1)
    own, other = x * (NY * block), (1 - x) * (NY * block)
    within = jnp.where(lane < block, own + lane, other + lane - block)
    parts = []
    for back in COLUMNS_BACK:
        column = lax.rem(y + NY - back, NY) * block
        tiles = []
        for layer_back in layers:
            at = within + ((z - layer_back) * (NX * NY * block) + column)
            tiles.append(jnp.where((at >= first) & (at <= last), 0.0, MASKED))
        parts.append(jnp.concatenate(tiles, axis=1))
    return parts


def attend_group(queries, kv_refs, bias, top, scale):
    size = queries.shape[1]
    scores = []
    for ref, part in zip(kv_refs, bias):
        keys = ref[0].reshape(-1, size)
        raw = lax.dot_general(queries, keys, (((1,), (1,)), ((), ())), preferred_element_type=jnp.float32)
        scores.append((raw.reshape(GROUP, -1, raw.shape[1]) + part[None]).reshape(raw.shape))
    highest = functools.reduce(jnp.maximum, [jnp.max(s, axis=1, keepdims=True) for s in scores])
    if top is not None:
        highest = jnp.maximum(highest, top)
    offset = highest * scale
    total, mixed = 0.0, 0.0
    for ref, s in zip(kv_refs, scores):
        kept = jnp.exp2(s * scale - offset)
        total = total + jnp.sum(kept, axis=1, keepdims=True)
        mixed = mixed + jnp.dot(kept.astype(jnp.bfloat16), ref[1].reshape(-1, size), preferred_element_type=jnp.float32)
    return highest, total, mixed


def near_kernel(heads, size, block, info, own_ref, other_ref, k0, k1, k2, k3, mixed_ref, stat_ref):
    scale = math.log2(math.e) / math.sqrt(size)
    lane = lax.broadcasted_iota(jnp.int32, (block, 128), 1)
    for which, query_ref in enumerate((own_ref, other_ref)):
        bias = bias_of(info, which, NEAR, block)
        stats = jnp.zeros((block, 128), jnp.float32)
        for start in range(0, heads, GROUP):
            group = range(start, start + GROUP)
            queries = jnp.concatenate([query_ref[:, h * size:(h + 1) * size] for h in group], axis=0)
            highest, total, mixed = attend_group(queries, (k0, k1, k2, k3), bias, None, scale)
            for i, head in enumerate(group):
                part = slice(i * block, (i + 1) * block)
                mixed_ref[which, :, head * size:(head + 1) * size] = mixed[part]
                stats = jnp.where(lane == head, highest[part], stats)
                stats = jnp.where(lane == heads + head, total[part], stats)
        stat_ref[which] = stats


def far_block(heads, size, block, which, info, query_ref, kv_refs, mixed_ref, stat_ref, context_ref):
    scale = math.log2(math.e) / math.sqrt(size)
    bias = bias_of(info, which, FAR, block)
    stats = stat_ref[which]
    for start in range(0, heads, GROUP):
        group = range(start, start + GROUP)
        queries = jnp.concatenate([query_ref[:, h * size:(h + 1) * size] for h in group], axis=0)
        old_top = jnp.concatenate([stats[:, h:h + 1] for h in group], axis=0)
        highest, total, mixed = attend_group(queries, kv_refs, bias, old_top, scale)
        fade = jnp.exp2((old_top - highest) * scale)
        for i, head in enumerate(group):
            part, at = slice(i * block, (i + 1) * block), slice(head * size, (head + 1) * size)
            whole = total[part] + stats[:, heads + head:heads + head + 1] * fade[part]
            context_ref[:, at] = ((mixed[part] + mixed_ref[which, :, at] * fade[part]) / whole).astype(jnp.bfloat16)


def far_kernel(heads, size, block, info, query_ref, k0, k1, k2, k3, mixed_ref, stat_ref, context_ref):
    far_block(heads, size, block, 1, info, query_ref, (k0, k1, k2, k3), mixed_ref, stat_ref, context_ref)


def project(core, own_half, context_ref, weight_ref, out_ref, pieces=1, piece=0):
    width = out_ref.shape[1]
    which = core if own_half else 1 - core
    columns = pl.ds(pl.multiple_of((which * pieces + piece) * width, width), width)
    out_ref[...] = jnp.dot(context_ref[...], weight_ref[:, columns], preferred_element_type=jnp.float32).astype(out_ref.dtype)


def project_kernel(own_half, info, context_ref, weight_ref, out_ref):
    project(info[3], own_half, context_ref, weight_ref, out_ref)


def far_project_kernel(heads, size, block, info, query_ref, k0, k1, k2, k3, mixed_ref, stat_ref, weight_ref, give0_ref, give1_ref, keep_ref, context_ref):
    far_block(heads, size, block, 0, info, query_ref, (k0, k1, k2, k3), mixed_ref, stat_ref, context_ref)
    project(info[3], False, context_ref, weight_ref, give0_ref, 2, 0)
    project(info[3], False, context_ref, weight_ref, give1_ref, 2, 1)
    project(info[3], True, context_ref, weight_ref, keep_ref)


def place_kernel(pieces, info, *refs):
    parts, out_ref, sems = refs[:4 * pieces], refs[-2], refs[-1]
    batch, core = info[8], info[3]
    width = parts[0].shape[1]
    copies = []
    for i, part in enumerate(parts):
        row = 1 - batch if (i // pieces) % 2 else batch
        half = 1 - core if i // pieces >= 2 else core
        at = pl.multiple_of(half * (pieces * width) + (i % pieces) * width, 128)
        copies.append(pltpu.make_async_copy(part, out_ref.at[row, :, pl.ds(at, width)], sems.at[i]))
    for copy in copies:
        copy.start()
    for copy in copies:
        copy.wait()


def body(queries, key_projected, values, segments, out_weight):
    batches, block, width = queries.shape
    size = key_projected.shape[2]
    heads = width // size
    features = out_weight.shape[1]
    seq, tp = lax.axis_index("seq"), lax.axis_index("tp")
    z, x, y = seq // (NX * NY), (seq // NY) % NX, seq % NY
    high, core = tp // NC, tp % NC
    batch = x ^ high
    pick = lambda a, i: lax.dynamic_index_in_dim(a, i, 0, keepdims=False)

    pair = jnp.stack([key_projected, values], axis=1)
    unit = jnp.concatenate([pick(pair, batch), swap_x(pick(pair, 1 - batch))], axis=1)
    back = {0: unit}
    for by in (1, 2, 3, 4):
        back[by] = shift_z(unit, by)
    near = jnp.stack([back[layer] for layer in NEAR], axis=1)
    far = jnp.stack([back[layer] for layer in FAR], axis=1)
    near_all = [near] + [shift_y(near, by) for by in COLUMNS_BACK[1:]]
    far_all = [far] + [shift_y(far, by) for by in COLUMNS_BACK[1:]]
    own_q = pick(queries, batch)
    other_q = swap_x(pick(queries, 1 - batch))

    seg = pick(segments, batch)
    starts = jnp.sum((seg[None, :] < jnp.arange(4, dtype=jnp.int32)[:, None]).astype(jnp.int32), axis=1)
    info = jnp.concatenate([jnp.stack([z, x, y, core]).astype(jnp.int32), starts, batch[None].astype(jnp.int32)])

    mixed, stats = pl.pallas_call(
        functools.partial(near_kernel, heads, size, block),
        out_shape=(
            jax.ShapeDtypeStruct((2, block, width), jnp.float32),
            jax.ShapeDtypeStruct((2, block, 128), jnp.float32),
        ),
        in_specs=[SMEM] + [VMEM] * 6,
        out_specs=(VMEM, VMEM),
        compiler_params=LIMIT,
        cost_estimate=LONG,
    )(info, own_q, other_q, *near_all)

    other_context = pl.pallas_call(
        functools.partial(far_kernel, heads, size, block),
        out_shape=jax.ShapeDtypeStruct((block, width), jnp.bfloat16),
        in_specs=[SMEM] + [VMEM] * 7,
        out_specs=VMEM,
        compiler_params=LIMIT,
        cost_estimate=LONG,
    )(info, other_q, *far_all, mixed, stats)

    def projected(own_half, dtype):
        return pl.pallas_call(
            functools.partial(project_kernel, own_half),
            out_shape=jax.ShapeDtypeStruct((block, features // 2), dtype),
            in_specs=[SMEM, VMEM, VMEM],
            out_specs=VMEM,
            compiler_params=LIMIT,
        )(info, other_context, out_weight)

    def cut(array):
        return jnp.split(array, PIECES, axis=1)

    given = swap_core(projected(False, jnp.bfloat16))
    sent = (projected(True, jnp.float32) + given.astype(jnp.float32)).astype(jnp.bfloat16)
    sent, own_q = lax.optimization_barrier((sent, own_q))
    arrived = [swap_both(piece) for piece in cut(sent)]
    given0, given1, kept = pl.pallas_call(
        functools.partial(far_project_kernel, heads, size, block),
        out_shape=(
            jax.ShapeDtypeStruct((block, features // 4), jnp.bfloat16),
            jax.ShapeDtypeStruct((block, features // 4), jnp.bfloat16),
            jax.ShapeDtypeStruct((block, features // 2), jnp.float32),
        ),
        in_specs=[SMEM] + [VMEM] * 8,
        out_specs=(VMEM, VMEM, VMEM),
        scratch_shapes=[pltpu.VMEM((block, width), jnp.bfloat16)],
        compiler_params=LIMIT,
    )(info, own_q, *far_all, mixed, stats, out_weight)
    given = jnp.concatenate([swap_core(given0), swap_core(given1)], axis=1)
    summed = kept + given.astype(jnp.float32)

    final = [(s + a.astype(jnp.float32)).astype(jnp.bfloat16) for s, a in zip(cut(summed), arrived)]
    other = [swap_high(f) for f in final]

    parts = final + other + [swap_core(f) for f in final] + [swap_core(o) for o in other]
    return pl.pallas_call(
        functools.partial(place_kernel, PIECES),
        out_shape=jax.ShapeDtypeStruct((batches, block, features), jnp.bfloat16),
        in_specs=[SMEM] + [VMEM] * len(parts),
        out_specs=HBM,
        scratch_shapes=[pltpu.SemaphoreType.DMA((len(parts),))],
        compiler_params=LIMIT,
    )(info, *parts)


def solution(mesh):
    in_specs = (
        P(None, "seq", "tp"),
        P(None, "seq", "tp"),
        P(None, "seq", "tp"),
        P(),
        P("tp", None),
    )
    return jax.shard_map(body, mesh=mesh, in_specs=in_specs, out_specs=P(None, "seq", None), check_vma=False)
```

```python
import functools
import math

import jax
import jax.numpy as jnp
from jax import lax
from jax.experimental import pallas as pl
from jax.experimental.pallas import tpu as pltpu
from jax.sharding import PartitionSpec as P

NZ, NX, NY, NH, NC = 8, 2, 4, 2, 2
AXES = ("seq", "tp")
MASKED = -1e30
NEAR, FAR = (0, 1, 2), (3, 4)
COLUMNS_BACK = (0, 1, 3, 2)
GROUP = 4
PIECES = 1
LONG = pl.CostEstimate(flops=16 << 30, bytes_accessed=16 << 20, transcendentals=4 << 20)
LIMIT = pltpu.CompilerParams(vmem_limit_bytes=24 * 1024 * 1024)
SMEM = pl.BlockSpec(memory_space=pltpu.SMEM)
VMEM = pl.BlockSpec(memory_space=pltpu.VMEM)
HBM = pl.BlockSpec(memory_space=pl.ANY)


def shift(array, move):
    flat = lambda z, x, y, h, c: (((z * NX + x) * NY + y) * NH + h) * NC + c
    devices = [
        (z, x, y, h, c)
        for z in range(NZ) for x in range(NX) for y in range(NY) for h in range(NH) for c in range(NC)
    ]
    return lax.ppermute(array, AXES, [(flat(*d), flat(*move(*d))) for d in devices])


def swap_x(array):
    return shift(array, lambda z, x, y, h, c: (z, 1 - x, y, h, c))


def swap_core(array):
    return shift(array, lambda z, x, y, h, c: (z, x, y, h, 1 - c))


def swap_high(array):
    return shift(array, lambda z, x, y, h, c: (z, x, y, 1 - h, c))


def swap_both(array):
    return shift(array, lambda z, x, y, h, c: (z, 1 - x, y, 1 - h, c))


def shift_z(array, by):
    return shift(array, lambda z, x, y, h, c: ((z + by) % NZ, x, y, h, c))


def shift_y(array, by):
    return shift(array, lambda z, x, y, h, c: (z, x, (y + by) % NY, h, c))


def row_limits(info, which, block):
    z, x, y = info[0], info[1], info[2]
    base = (z * NX + (1 - x if which else x)) * (NY * block) + y * block
    last = base + lax.broadcasted_iota(jnp.int32, (block, 1), 0)
    first = jnp.zeros_like(last)
    for at in range(4):
        start = info[4 + at]
        first = jnp.where(start <= last, jnp.maximum(first, start), first)
    return first, last


def bias_of(info, which, layers, block):
    z, x, y = info[0], info[1], info[2]
    first, last = row_limits(info, which, block)
    lane = lax.broadcasted_iota(jnp.int32, (1, 2 * block), 1)
    own, other = x * (NY * block), (1 - x) * (NY * block)
    within = jnp.where(lane < block, own + lane, other + lane - block)
    parts = []
    for back in COLUMNS_BACK:
        column = lax.rem(y + NY - back, NY) * block
        tiles = []
        for layer_back in layers:
            at = within + ((z - layer_back) * (NX * NY * block) + column)
            tiles.append(jnp.where((at >= first) & (at <= last), 0.0, MASKED))
        parts.append(jnp.concatenate(tiles, axis=1))
    return parts


def attend_group(queries, kv_refs, bias, top, scale):
    size = queries.shape[1]
    scores = []
    for ref, part in zip(kv_refs, bias):
        keys = ref[0].reshape(-1, size)
        raw = lax.dot_general(queries, keys, (((1,), (1,)), ((), ())), preferred_element_type=jnp.float32)
        scores.append((raw.reshape(GROUP, -1, raw.shape[1]) + part[None]).reshape(raw.shape))
    highest = functools.reduce(jnp.maximum, [jnp.max(s, axis=1, keepdims=True) for s in scores])
    if top is not None:
        highest = jnp.maximum(highest, top)
    offset = highest * scale
    total, mixed = 0.0, 0.0
    for ref, s in zip(kv_refs, scores):
        kept = jnp.exp2(s * scale - offset)
        total = total + jnp.sum(kept, axis=1, keepdims=True)
        mixed = mixed + jnp.dot(kept.astype(jnp.bfloat16), ref[1].reshape(-1, size), preferred_element_type=jnp.float32)
    return highest, total, mixed


def near_kernel(heads, size, block, info, own_ref, other_ref, k0, k1, k2, k3, mixed_ref, stat_ref):
    scale = math.log2(math.e) / math.sqrt(size)
    lane = lax.broadcasted_iota(jnp.int32, (block, 128), 1)
    for which, query_ref in enumerate((own_ref, other_ref)):
        bias = bias_of(info, which, NEAR, block)
        stats = jnp.zeros((block, 128), jnp.float32)
        for start in range(0, heads, GROUP):
            group = range(start, start + GROUP)
            queries = jnp.concatenate([query_ref[:, h * size:(h + 1) * size] for h in group], axis=0)
            highest, total, mixed = attend_group(queries, (k0, k1, k2, k3), bias, None, scale)
            for i, head in enumerate(group):
                part = slice(i * block, (i + 1) * block)
                mixed_ref[which, :, head * size:(head + 1) * size] = mixed[part]
                stats = jnp.where(lane == head, highest[part], stats)
                stats = jnp.where(lane == heads + head, total[part], stats)
        stat_ref[which] = stats


def far_block(heads, size, block, which, info, query_ref, kv_refs, mixed_ref, stat_ref, context_ref):
    scale = math.log2(math.e) / math.sqrt(size)
    bias = bias_of(info, which, FAR, block)
    stats = stat_ref[which]
    for start in range(0, heads, GROUP):
        group = range(start, start + GROUP)
        queries = jnp.concatenate([query_ref[:, h * size:(h + 1) * size] for h in group], axis=0)
        old_top = jnp.concatenate([stats[:, h:h + 1] for h in group], axis=0)
        highest, total, mixed = attend_group(queries, kv_refs, bias, old_top, scale)
        fade = jnp.exp2((old_top - highest) * scale)
        for i, head in enumerate(group):
            part, at = slice(i * block, (i + 1) * block), slice(head * size, (head + 1) * size)
            whole = total[part] + stats[:, heads + head:heads + head + 1] * fade[part]
            context_ref[:, at] = ((mixed[part] + mixed_ref[which, :, at] * fade[part]) / whole).astype(jnp.bfloat16)


def far_kernel(heads, size, block, info, query_ref, k0, k1, k2, k3, mixed_ref, stat_ref, context_ref):
    far_block(heads, size, block, 1, info, query_ref, (k0, k1, k2, k3), mixed_ref, stat_ref, context_ref)


def project(core, own_half, context_ref, weight_ref, out_ref, pieces=1, piece=0):
    width = out_ref.shape[1]
    which = core if own_half else 1 - core
    columns = pl.ds(pl.multiple_of((which * pieces + piece) * width, width), width)
    out_ref[...] = jnp.dot(context_ref[...], weight_ref[:, columns], preferred_element_type=jnp.float32).astype(out_ref.dtype)


def project_kernel(own_half, info, context_ref, weight_ref, out_ref):
    project(info[3], own_half, context_ref, weight_ref, out_ref)


def far_project_kernel(heads, size, block, info, query_ref, k0, k1, k2, k3, mixed_ref, stat_ref, weight_ref, give0_ref, give1_ref, keep_ref, context_ref):
    far_block(heads, size, block, 0, info, query_ref, (k0, k1, k2, k3), mixed_ref, stat_ref, context_ref)
    project(info[3], False, context_ref, weight_ref, give0_ref, 2, 0)
    project(info[3], False, context_ref, weight_ref, give1_ref, 2, 1)
    project(info[3], True, context_ref, weight_ref, keep_ref)


def place_kernel(pieces, info, *refs):
    parts, out_ref, sems = refs[:4 * pieces], refs[-2], refs[-1]
    batch, core = info[8], info[3]
    width = parts[0].shape[1]
    copies = []
    for i, part in enumerate(parts):
        row = 1 - batch if (i // pieces) % 2 else batch
        half = 1 - core if i // pieces >= 2 else core
        at = pl.multiple_of(half * (pieces * width) + (i % pieces) * width, 128)
        copies.append(pltpu.make_async_copy(part, out_ref.at[row, :, pl.ds(at, width)], sems.at[i]))
    for copy in copies:
        copy.start()
    for copy in copies:
        copy.wait()


def body(queries, key_projected, values, segments, out_weight):
    batches, block, width = queries.shape
    size = key_projected.shape[2]
    heads = width // size
    features = out_weight.shape[1]
    seq, tp = lax.axis_index("seq"), lax.axis_index("tp")
    z, x, y = seq // (NX * NY), (seq // NY) % NX, seq % NY
    high, core = tp // NC, tp % NC
    batch = x ^ high
    pick = lambda a, i: lax.dynamic_index_in_dim(a, i, 0, keepdims=False)

    pair = jnp.stack([key_projected, values], axis=1)
    unit = jnp.concatenate([pick(pair, batch), swap_x(pick(pair, 1 - batch))], axis=1)
    back = {0: unit}
    for by in (1, 2, 3, 4):
        back[by] = shift_z(unit, by)
    near = jnp.stack([back[layer] for layer in NEAR], axis=1)
    far = jnp.stack([back[layer] for layer in FAR], axis=1)
    near_all = [near] + [shift_y(near, by) for by in COLUMNS_BACK[1:]]
    far_all = [far] + [shift_y(far, by) for by in COLUMNS_BACK[1:]]
    own_q = pick(queries, batch)
    other_q = swap_x(pick(queries, 1 - batch))

    seg = pick(segments, batch)
    starts = jnp.sum((seg[None, :] < jnp.arange(4, dtype=jnp.int32)[:, None]).astype(jnp.int32), axis=1)
    info = jnp.concatenate([jnp.stack([z, x, y, core]).astype(jnp.int32), starts, batch[None].astype(jnp.int32)])

    mixed, stats = pl.pallas_call(
        functools.partial(near_kernel, heads, size, block),
        out_shape=(
            jax.ShapeDtypeStruct((2, block, width), jnp.float32),
            jax.ShapeDtypeStruct((2, block, 128), jnp.float32),
        ),
        in_specs=[SMEM] + [VMEM] * 6,
        out_specs=(VMEM, VMEM),
        compiler_params=LIMIT,
        cost_estimate=LONG,
    )(info, own_q, other_q, *near_all)

    other_context = pl.pallas_call(
        functools.partial(far_kernel, heads, size, block),
        out_shape=jax.ShapeDtypeStruct((block, width), jnp.bfloat16),
        in_specs=[SMEM] + [VMEM] * 7,
        out_specs=VMEM,
        compiler_params=LIMIT,
        cost_estimate=LONG,
    )(info, other_q, *far_all, mixed, stats)

    def projected(own_half, dtype):
        return pl.pallas_call(
            functools.partial(project_kernel, own_half),
            out_shape=jax.ShapeDtypeStruct((block, features // 2), dtype),
            in_specs=[SMEM, VMEM, VMEM],
            out_specs=VMEM,
            compiler_params=LIMIT,
        )(info, other_context, out_weight)

    def cut(array):
        return jnp.split(array, PIECES, axis=1)

    given = swap_core(projected(False, jnp.bfloat16))
    sent = (projected(True, jnp.float32) + given.astype(jnp.float32)).astype(jnp.bfloat16)
    sent, own_q = lax.optimization_barrier((sent, own_q))
    arrived = [swap_both(piece) for piece in cut(sent)]
    given0, given1, kept = pl.pallas_call(
        functools.partial(far_project_kernel, heads, size, block),
        out_shape=(
            jax.ShapeDtypeStruct((block, features // 4), jnp.bfloat16),
            jax.ShapeDtypeStruct((block, features // 4), jnp.bfloat16),
            jax.ShapeDtypeStruct((block, features // 2), jnp.float32),
        ),
        in_specs=[SMEM] + [VMEM] * 8,
        out_specs=(VMEM, VMEM, VMEM),
        scratch_shapes=[pltpu.VMEM((block, width), jnp.bfloat16)],
        compiler_params=LIMIT,
    )(info, own_q, *far_all, mixed, stats, out_weight)
    given = jnp.concatenate([swap_core(given0), swap_core(given1)], axis=1)
    summed = kept + given.astype(jnp.float32)

    final = [(s + a.astype(jnp.float32)).astype(jnp.bfloat16) for s, a in zip(cut(summed), arrived)]
    other = [swap_high(f) for f in final]

    parts = final + other + [swap_core(f) for f in final] + [swap_core(o) for o in other]
    return pl.pallas_call(
        functools.partial(place_kernel, PIECES),
        out_shape=jax.ShapeDtypeStruct((batches, block, features), jnp.bfloat16),
        in_specs=[SMEM] + [VMEM] * len(parts),
        out_specs=HBM,
        scratch_shapes=[pltpu.SemaphoreType.DMA((len(parts),))],
        compiler_params=LIMIT,
    )(info, *parts)


def solution(mesh):
    in_specs = (
        P(None, "seq", "tp"),
        P(None, "seq", "tp"),
        P(None, "seq", "tp"),
        P(),
        P("tp", None),
    )
    return jax.shard_map(body, mesh=mesh, in_specs=in_specs, out_specs=P(None, "seq", None), check_vma=False)
```

```python
import functools
import math

import jax
import jax.numpy as jnp
from jax import lax
from jax.experimental import pallas as pl
from jax.experimental.pallas import tpu as pltpu
from jax.sharding import PartitionSpec as P

NZ, NX, NY, NH, NC = 8, 2, 4, 2, 2
AXES = ("seq", "tp")
MASKED = -1e30
NEAR, FAR = (0, 1, 2), (3, 4)
COLUMNS_BACK = (0, 1, 3, 2)
GROUP = 4
PIECES = 1
LONG = pl.CostEstimate(flops=16 << 30, bytes_accessed=16 << 20, transcendentals=4 << 20)
LIMIT = pltpu.CompilerParams(vmem_limit_bytes=24 * 1024 * 1024)
VMEM = pl.BlockSpec(memory_space=pltpu.VMEM)
HBM = pl.BlockSpec(memory_space=pl.ANY)


def shift(array, move):
    flat = lambda z, x, y, h, c: (((z * NX + x) * NY + y) * NH + h) * NC + c
    devices = [
        (z, x, y, h, c)
        for z in range(NZ) for x in range(NX) for y in range(NY) for h in range(NH) for c in range(NC)
    ]
    return lax.ppermute(array, AXES, [(flat(*d), flat(*move(*d))) for d in devices])


def swap_x(array):
    return shift(array, lambda z, x, y, h, c: (z, 1 - x, y, h, c))


def swap_core(array):
    return shift(array, lambda z, x, y, h, c: (z, x, y, h, 1 - c))


def swap_high(array):
    return shift(array, lambda z, x, y, h, c: (z, x, y, 1 - h, c))


def swap_both(array):
    return shift(array, lambda z, x, y, h, c: (z, 1 - x, y, 1 - h, c))


def shift_z(array, by):
    return shift(array, lambda z, x, y, h, c: ((z + by) % NZ, x, y, h, c))


def shift_y(array, by):
    return shift(array, lambda z, x, y, h, c: (z, x, (y + by) % NY, h, c))


def coordinates():
    seq, tp = lax.axis_index("seq"), lax.axis_index("tp")
    return seq // (NX * NY), (seq // NY) % NX, seq % NY, tp // NC, tp % NC


def row_positions(which, block):
    z, x, y, _, _ = coordinates()
    base = (z * NX + (1 - x if which else x)) * (NY * block) + y * block
    return base + lax.broadcasted_iota(jnp.int32, (block, 1), 0)


def bias_of(first_ref, which, layers, block):
    z, x, y, _, _ = coordinates()
    first, last = first_ref[which, :, :1], row_positions(which, block)
    lane = lax.broadcasted_iota(jnp.int32, (1, 2 * block), 1)
    own, other = x * (NY * block), (1 - x) * (NY * block)
    within = jnp.where(lane < block, own + lane, other + lane - block)
    parts = []
    for back in COLUMNS_BACK:
        column = lax.rem(y + NY - back, NY) * block
        tiles = []
        for layer_back in layers:
            at = within + ((z - layer_back) * (NX * NY * block) + column)
            tiles.append(jnp.where((at >= first) & (at <= last), 0.0, MASKED))
        parts.append(jnp.concatenate(tiles, axis=1))
    return parts


def attend_group(queries, kv_refs, bias, top, scale):
    size = queries.shape[1]
    scores = []
    for ref, part in zip(kv_refs, bias):
        keys = ref[0].reshape(-1, size)
        raw = lax.dot_general(queries, keys, (((1,), (1,)), ((), ())), preferred_element_type=jnp.float32)
        scores.append((raw.reshape(GROUP, -1, raw.shape[1]) + part[None]).reshape(raw.shape))
    highest = functools.reduce(jnp.maximum, [jnp.max(s, axis=1, keepdims=True) for s in scores])
    if top is not None:
        highest = jnp.maximum(highest, top)
    offset = highest * scale
    total, mixed = 0.0, 0.0
    for ref, s in zip(kv_refs, scores):
        kept = jnp.exp2(s * scale - offset)
        total = total + jnp.sum(kept, axis=1, keepdims=True)
        mixed = mixed + jnp.dot(kept.astype(jnp.bfloat16), ref[1].reshape(-1, size), preferred_element_type=jnp.float32)
    return highest, total, mixed


def near_kernel(heads, size, block, first_ref, own_ref, other_ref, k0, k1, k2, k3, mixed_ref, stat_ref):
    scale = math.log2(math.e) / math.sqrt(size)
    lane = lax.broadcasted_iota(jnp.int32, (block, 128), 1)
    for which, query_ref in enumerate((own_ref, other_ref)):
        bias = bias_of(first_ref, which, NEAR, block)
        stats = jnp.zeros((block, 128), jnp.float32)
        for start in range(0, heads, GROUP):
            group = range(start, start + GROUP)
            queries = jnp.concatenate([query_ref[:, h * size:(h + 1) * size] for h in group], axis=0)
            highest, total, mixed = attend_group(queries, (k0, k1, k2, k3), bias, None, scale)
            for i, head in enumerate(group):
                part = slice(i * block, (i + 1) * block)
                mixed_ref[which, :, head * size:(head + 1) * size] = mixed[part]
                stats = jnp.where(lane == head, highest[part], stats)
                stats = jnp.where(lane == heads + head, total[part], stats)
        stat_ref[which] = stats


def far_block(heads, size, block, which, first_ref, query_ref, kv_refs, mixed_ref, stat_ref, context_ref):
    scale = math.log2(math.e) / math.sqrt(size)
    bias = bias_of(first_ref, which, FAR, block)
    stats = stat_ref[which]
    for start in range(0, heads, GROUP):
        group = range(start, start + GROUP)
        queries = jnp.concatenate([query_ref[:, h * size:(h + 1) * size] for h in group], axis=0)
        old_top = jnp.concatenate([stats[:, h:h + 1] for h in group], axis=0)
        highest, total, mixed = attend_group(queries, kv_refs, bias, old_top, scale)
        fade = jnp.exp2((old_top - highest) * scale)
        for i, head in enumerate(group):
            part, at = slice(i * block, (i + 1) * block), slice(head * size, (head + 1) * size)
            whole = total[part] + stats[:, heads + head:heads + head + 1] * fade[part]
            context_ref[:, at] = ((mixed[part] + mixed_ref[which, :, at] * fade[part]) / whole).astype(jnp.bfloat16)


def far_kernel(heads, size, block, first_ref, query_ref, k0, k1, k2, k3, mixed_ref, stat_ref, context_ref):
    far_block(heads, size, block, 1, first_ref, query_ref, (k0, k1, k2, k3), mixed_ref, stat_ref, context_ref)


def project(own_half, context_ref, weight_ref, out_ref, pieces=1, piece=0):
    width = out_ref.shape[1]
    core = coordinates()[-1]
    which = core if own_half else 1 - core
    columns = pl.ds(pl.multiple_of((which * pieces + piece) * width, width), width)
    out_ref[...] = jnp.dot(context_ref[...], weight_ref[:, columns], preferred_element_type=jnp.float32).astype(out_ref.dtype)


def project_kernel(own_half, context_ref, weight_ref, out_ref):
    project(own_half, context_ref, weight_ref, out_ref)


def far_project_kernel(heads, size, block, first_ref, query_ref, k0, k1, k2, k3, mixed_ref, stat_ref, weight_ref, give0_ref, give1_ref, keep_ref, context_ref):
    far_block(heads, size, block, 0, first_ref, query_ref, (k0, k1, k2, k3), mixed_ref, stat_ref, context_ref)
    project(False, context_ref, weight_ref, give0_ref, 2, 0)
    project(False, context_ref, weight_ref, give1_ref, 2, 1)
    project(True, context_ref, weight_ref, keep_ref)


def place_kernel(pieces, *refs):
    parts, out_ref, sems = refs[:4 * pieces], refs[-2], refs[-1]
    _, x, _, high, core = coordinates()
    batch = x ^ high
    width = parts[0].shape[1]
    copies = []
    for i, part in enumerate(parts):
        row = 1 - batch if (i // pieces) % 2 else batch
        half = 1 - core if i // pieces >= 2 else core
        at = pl.multiple_of(half * (pieces * width) + (i % pieces) * width, 128)
        copies.append(pltpu.make_async_copy(part, out_ref.at[row, :, pl.ds(at, width)], sems.at[i]))
    for copy in copies:
        copy.start()
    for copy in copies:
        copy.wait()


def body(queries, key_projected, values, segments, out_weight):
    batches, block, width = queries.shape
    size = key_projected.shape[2]
    heads = width // size
    features = out_weight.shape[1]
    z, x, y, high, core = coordinates()
    batch = x ^ high
    pick = lambda a, i: lax.dynamic_index_in_dim(a, i, 0, keepdims=False)

    pair = jnp.stack([key_projected, values], axis=1)
    unit = jnp.concatenate([pick(pair, batch), swap_x(pick(pair, 1 - batch))], axis=1)
    back = {0: unit}
    for by in (1, 2, 3, 4):
        back[by] = shift_z(unit, by)
    near = jnp.stack([back[layer] for layer in NEAR], axis=1)
    far = jnp.stack([back[layer] for layer in FAR], axis=1)
    near_all = [near] + [shift_y(near, by) for by in COLUMNS_BACK[1:]]
    far_all = [far] + [shift_y(far, by) for by in COLUMNS_BACK[1:]]
    own_q = pick(queries, batch)
    other_q = swap_x(pick(queries, 1 - batch))

    seg = pick(segments, batch)
    starts = jnp.sum((seg[None, :] < jnp.arange(4, dtype=jnp.int32)[:, None]).astype(jnp.int32), axis=1)
    positions = jnp.stack([row_positions(which, block) for which in (0, 1)])
    first = jnp.max(jnp.where(starts <= positions, starts, 0), axis=2, keepdims=True)
    first = jnp.broadcast_to(first, (2, block, 128))

    mixed, stats = pl.pallas_call(
        functools.partial(near_kernel, heads, size, block),
        out_shape=(
            jax.ShapeDtypeStruct((2, block, width), jnp.float32),
            jax.ShapeDtypeStruct((2, block, 128), jnp.float32),
        ),
        in_specs=[VMEM] * 7,
        out_specs=(VMEM, VMEM),
        compiler_params=LIMIT,
        cost_estimate=LONG,
    )(first, own_q, other_q, *near_all)

    other_context = pl.pallas_call(
        functools.partial(far_kernel, heads, size, block),
        out_shape=jax.ShapeDtypeStruct((block, width), jnp.bfloat16),
        in_specs=[VMEM] * 8,
        out_specs=VMEM,
        compiler_params=LIMIT,
        cost_estimate=LONG,
    )(first, other_q, *far_all, mixed, stats)

    def projected(own_half, dtype):
        return pl.pallas_call(
            functools.partial(project_kernel, own_half),
            out_shape=jax.ShapeDtypeStruct((block, features // 2), dtype),
            in_specs=[VMEM, VMEM],
            out_specs=VMEM,
            compiler_params=LIMIT,
        )(other_context, out_weight)

    def cut(array):
        return jnp.split(array, PIECES, axis=1)

    given = swap_core(projected(False, jnp.bfloat16))
    sent = (projected(True, jnp.float32) + given.astype(jnp.float32)).astype(jnp.bfloat16)
    sent, own_q = lax.optimization_barrier((sent, own_q))
    arrived = [swap_both(piece) for piece in cut(sent)]
    given0, given1, kept = pl.pallas_call(
        functools.partial(far_project_kernel, heads, size, block),
        out_shape=(
            jax.ShapeDtypeStruct((block, features // 4), jnp.bfloat16),
            jax.ShapeDtypeStruct((block, features // 4), jnp.bfloat16),
            jax.ShapeDtypeStruct((block, features // 2), jnp.float32),
        ),
        in_specs=[VMEM] * 9,
        out_specs=(VMEM, VMEM, VMEM),
        scratch_shapes=[pltpu.VMEM((block, width), jnp.bfloat16)],
        compiler_params=LIMIT,
    )(first, own_q, *far_all, mixed, stats, out_weight)
    given = jnp.concatenate([swap_core(given0), swap_core(given1)], axis=1)
    summed = kept + given.astype(jnp.float32)

    final = [(s + a.astype(jnp.float32)).astype(jnp.bfloat16) for s, a in zip(cut(summed), arrived)]
    other = [swap_high(f) for f in final]

    parts = final + other + [swap_core(f) for f in final] + [swap_core(o) for o in other]
    return pl.pallas_call(
        functools.partial(place_kernel, PIECES),
        out_shape=jax.ShapeDtypeStruct((batches, block, features), jnp.bfloat16),
        in_specs=[VMEM] * len(parts),
        out_specs=HBM,
        scratch_shapes=[pltpu.SemaphoreType.DMA((len(parts),))],
        compiler_params=LIMIT,
    )(*parts)


def solution(mesh):
    in_specs = (
        P(None, "seq", "tp"),
        P(None, "seq", "tp"),
        P(None, "seq", "tp"),
        P(),
        P("tp", None),
    )
    return jax.shard_map(body, mesh=mesh, in_specs=in_specs, out_specs=P(None, "seq", None), check_vma=False)
```

```python
import functools
import math

import jax
import jax.numpy as jnp
from jax import lax
from jax.experimental import pallas as pl
from jax.experimental.pallas import tpu as pltpu
from jax.sharding import PartitionSpec as P

NZ, NX, NY, NH, NC = 8, 2, 4, 2, 2
AXES = ("seq", "tp")
MASKED = -1e30
NEAR, FAR = (0, 1, 2), (3, 4)
COLUMNS_BACK = (0, 1, 3, 2)
GROUP = 4
PIECES = 1
LONG = pl.CostEstimate(flops=16 << 30, bytes_accessed=16 << 20, transcendentals=4 << 20)
LIMIT = pltpu.CompilerParams(vmem_limit_bytes=24 * 1024 * 1024)
VMEM = pl.BlockSpec(memory_space=pltpu.VMEM)
HBM = pl.BlockSpec(memory_space=pl.ANY)


def shift(array, move):
    flat = lambda z, x, y, h, c: (((z * NX + x) * NY + y) * NH + h) * NC + c
    devices = [
        (z, x, y, h, c)
        for z in range(NZ) for x in range(NX) for y in range(NY) for h in range(NH) for c in range(NC)
    ]
    return lax.ppermute(array, AXES, [(flat(*d), flat(*move(*d))) for d in devices])


def swap_x(array):
    return shift(array, lambda z, x, y, h, c: (z, 1 - x, y, h, c))


def swap_core(array):
    return shift(array, lambda z, x, y, h, c: (z, x, y, h, 1 - c))


def swap_high(array):
    return shift(array, lambda z, x, y, h, c: (z, x, y, 1 - h, c))


def swap_both(array):
    return shift(array, lambda z, x, y, h, c: (z, 1 - x, y, 1 - h, c))


def shift_z(array, by):
    return shift(array, lambda z, x, y, h, c: ((z + by) % NZ, x, y, h, c))


def shift_y(array, by):
    return shift(array, lambda z, x, y, h, c: (z, x, (y + by) % NY, h, c))


def coordinates():
    seq, tp = lax.axis_index("seq"), lax.axis_index("tp")
    return seq // (NX * NY), (seq // NY) % NX, seq % NY, tp // NC, tp % NC


def row_positions(which, block):
    z, x, y, _, _ = coordinates()
    base = (z * NX + (1 - x if which else x)) * (NY * block) + y * block
    return base + lax.broadcasted_iota(jnp.int32, (block, 1), 0)


def bias_of(first_ref, which, layers, block):
    z, x, y, _, _ = coordinates()
    first, last = first_ref[which, :, :1], row_positions(which, block)
    lane = lax.broadcasted_iota(jnp.int32, (1, 2 * block), 1)
    own, other = x * (NY * block), (1 - x) * (NY * block)
    within = jnp.where(lane < block, own + lane, other + lane - block)
    parts = []
    for back in COLUMNS_BACK:
        column = lax.rem(y + NY - back, NY) * block
        tiles = []
        for layer_back in layers:
            at = within + ((z - layer_back) * (NX * NY * block) + column)
            tiles.append(jnp.where((at >= first) & (at <= last), 0.0, MASKED))
        parts.append(jnp.concatenate(tiles, axis=1))
    return parts


def attend_group(queries, kv_refs, bias, top, scale):
    size = queries.shape[1]
    scores = []
    for ref, part in zip(kv_refs, bias):
        keys = ref[0].reshape(-1, size)
        raw = lax.dot_general(queries, keys, (((1,), (1,)), ((), ())), preferred_element_type=jnp.float32)
        scores.append((raw.reshape(GROUP, -1, raw.shape[1]) + part[None]).reshape(raw.shape))
    highest = functools.reduce(jnp.maximum, [jnp.max(s, axis=1, keepdims=True) for s in scores])
    if top is not None:
        highest = jnp.maximum(highest, top)
    offset = highest * scale
    total, mixed = 0.0, 0.0
    for ref, s in zip(kv_refs, scores):
        kept = jnp.exp2(s * scale - offset)
        total = total + jnp.sum(kept, axis=1, keepdims=True)
        mixed = mixed + jnp.dot(kept.astype(jnp.bfloat16), ref[1].reshape(-1, size), preferred_element_type=jnp.float32)
    return highest, total, mixed


def near_kernel(heads, size, block, first_ref, own_ref, other_ref, k0, k1, k2, k3, mixed_ref, stat_ref):
    scale = math.log2(math.e) / math.sqrt(size)
    lane = lax.broadcasted_iota(jnp.int32, (block, 128), 1)
    for which, query_ref in enumerate((own_ref, other_ref)):
        bias = bias_of(first_ref, which, NEAR, block)
        stats = jnp.zeros((block, 128), jnp.float32)
        for start in range(0, heads, GROUP):
            group = range(start, start + GROUP)
            queries = jnp.concatenate([query_ref[:, h * size:(h + 1) * size] for h in group], axis=0)
            highest, total, mixed = attend_group(queries, (k0, k1, k2, k3), bias, None, scale)
            for i, head in enumerate(group):
                part = slice(i * block, (i + 1) * block)
                mixed_ref[which, :, head * size:(head + 1) * size] = mixed[part]
                stats = jnp.where(lane == head, highest[part], stats)
                stats = jnp.where(lane == heads + head, total[part], stats)
        stat_ref[which] = stats


def far_block(heads, size, block, which, first_ref, query_ref, kv_refs, mixed_ref, stat_ref, context_ref):
    scale = math.log2(math.e) / math.sqrt(size)
    bias = bias_of(first_ref, which, FAR, block)
    stats = stat_ref[which]
    for start in range(0, heads, GROUP):
        group = range(start, start + GROUP)
        queries = jnp.concatenate([query_ref[:, h * size:(h + 1) * size] for h in group], axis=0)
        old_top = jnp.concatenate([stats[:, h:h + 1] for h in group], axis=0)
        highest, total, mixed = attend_group(queries, kv_refs, bias, old_top, scale)
        fade = jnp.exp2((old_top - highest) * scale)
        for i, head in enumerate(group):
            part, at = slice(i * block, (i + 1) * block), slice(head * size, (head + 1) * size)
            whole = total[part] + stats[:, heads + head:heads + head + 1] * fade[part]
            context_ref[:, at] = ((mixed[part] + mixed_ref[which, :, at] * fade[part]) / whole).astype(jnp.bfloat16)


def far_kernel(heads, size, block, first_ref, query_ref, k0, k1, k2, k3, mixed_ref, stat_ref, context_ref):
    far_block(heads, size, block, 1, first_ref, query_ref, (k0, k1, k2, k3), mixed_ref, stat_ref, context_ref)


def project(own_half, context_ref, weight_ref, out_ref, pieces=1, piece=0):
    width = out_ref.shape[1]
    core = coordinates()[-1]
    which = core if own_half else 1 - core
    columns = pl.ds(pl.multiple_of((which * pieces + piece) * width, width), width)
    out_ref[...] = jnp.dot(context_ref[...], weight_ref[:, columns], preferred_element_type=jnp.float32).astype(out_ref.dtype)


def project_kernel(own_half, context_ref, weight_ref, out_ref):
    project(own_half, context_ref, weight_ref, out_ref)


def far_project_kernel(heads, size, block, first_ref, query_ref, k0, k1, k2, k3, mixed_ref, stat_ref, weight_ref, give0_ref, give1_ref, keep_ref, context_ref):
    far_block(heads, size, block, 0, first_ref, query_ref, (k0, k1, k2, k3), mixed_ref, stat_ref, context_ref)
    project(False, context_ref, weight_ref, give0_ref, 2, 0)
    project(False, context_ref, weight_ref, give1_ref, 2, 1)
    project(True, context_ref, weight_ref, keep_ref)


def place_kernel(pieces, *refs):
    parts, out_ref, sems = refs[:4 * pieces], refs[-2], refs[-1]
    _, x, _, high, core = coordinates()
    batch = x ^ high
    width = parts[0].shape[1]
    copies = []
    for i, part in enumerate(parts):
        row = 1 - batch if (i // pieces) % 2 else batch
        half = 1 - core if i // pieces >= 2 else core
        at = pl.multiple_of(half * (pieces * width) + (i % pieces) * width, 128)
        copies.append(pltpu.make_async_copy(part, out_ref.at[row, :, pl.ds(at, width)], sems.at[i]))
    for copy in copies:
        copy.start()
    for copy in copies:
        copy.wait()


def body(queries, key_projected, values, segments, out_weight):
    batches, block, width = queries.shape
    size = key_projected.shape[2]
    heads = width // size
    features = out_weight.shape[1]
    z, x, y, high, core = coordinates()
    batch = x ^ high
    pick = lambda a, i: lax.dynamic_index_in_dim(a, i, 0, keepdims=False)

    pair = jnp.stack([key_projected, values], axis=1)
    unit = jnp.concatenate([pick(pair, batch), swap_x(pick(pair, 1 - batch))], axis=1)
    back = {0: unit}
    for by in (1, 2, 3, 4):
        back[by] = shift_z(unit, by)
    near = jnp.stack([back[layer] for layer in NEAR], axis=1)
    far = jnp.stack([back[layer] for layer in FAR], axis=1)
    near_all = [near] + [shift_y(near, by) for by in COLUMNS_BACK[1:]]
    far_all = [far] + [shift_y(far, by) for by in COLUMNS_BACK[1:]]
    own_q = pick(queries, batch)
    other_q = swap_x(pick(queries, 1 - batch))

    seg = pick(segments, batch)
    starts = jnp.sum((seg[None, :] < jnp.arange(4, dtype=jnp.int32)[:, None]).astype(jnp.int32), axis=1)
    positions = jnp.stack([row_positions(which, block) for which in (0, 1)])
    first = jnp.max(jnp.where(starts <= positions, starts, 0), axis=2, keepdims=True)
    first = jnp.broadcast_to(first, (2, block, 128))

    mixed, stats = pl.pallas_call(
        functools.partial(near_kernel, heads, size, block),
        out_shape=(
            jax.ShapeDtypeStruct((2, block, width), jnp.float32),
            jax.ShapeDtypeStruct((2, block, 128), jnp.float32),
        ),
        in_specs=[VMEM] * 7,
        out_specs=(VMEM, VMEM),
        compiler_params=LIMIT,
        cost_estimate=LONG,
    )(first, own_q, other_q, *near_all)

    other_context = pl.pallas_call(
        functools.partial(far_kernel, heads, size, block),
        out_shape=jax.ShapeDtypeStruct((block, width), jnp.bfloat16),
        in_specs=[VMEM] * 8,
        out_specs=VMEM,
        compiler_params=LIMIT,
    )(first, other_q, *far_all, mixed, stats)

    def projected(own_half, dtype):
        return pl.pallas_call(
            functools.partial(project_kernel, own_half),
            out_shape=jax.ShapeDtypeStruct((block, features // 2), dtype),
            in_specs=[VMEM, VMEM],
            out_specs=VMEM,
            compiler_params=LIMIT,
        )(other_context, out_weight)

    def cut(array):
        return jnp.split(array, PIECES, axis=1)

    given = swap_core(projected(False, jnp.bfloat16))
    sent = (projected(True, jnp.float32) + given.astype(jnp.float32)).astype(jnp.bfloat16)
    sent, own_q = lax.optimization_barrier((sent, own_q))
    arrived = [swap_both(piece) for piece in cut(sent)]
    given0, given1, kept = pl.pallas_call(
        functools.partial(far_project_kernel, heads, size, block),
        out_shape=(
            jax.ShapeDtypeStruct((block, features // 4), jnp.bfloat16),
            jax.ShapeDtypeStruct((block, features // 4), jnp.bfloat16),
            jax.ShapeDtypeStruct((block, features // 2), jnp.float32),
        ),
        in_specs=[VMEM] * 9,
        out_specs=(VMEM, VMEM, VMEM),
        scratch_shapes=[pltpu.VMEM((block, width), jnp.bfloat16)],
        compiler_params=LIMIT,
    )(first, own_q, *far_all, mixed, stats, out_weight)
    given = jnp.concatenate([swap_core(given0), swap_core(given1)], axis=1)
    summed = kept + given.astype(jnp.float32)

    final = [(s + a.astype(jnp.float32)).astype(jnp.bfloat16) for s, a in zip(cut(summed), arrived)]
    other = [swap_high(f) for f in final]

    parts = final + other + [swap_core(f) for f in final] + [swap_core(o) for o in other]
    return pl.pallas_call(
        functools.partial(place_kernel, PIECES),
        out_shape=jax.ShapeDtypeStruct((batches, block, features), jnp.bfloat16),
        in_specs=[VMEM] * len(parts),
        out_specs=HBM,
        scratch_shapes=[pltpu.SemaphoreType.DMA((len(parts),))],
        compiler_params=LIMIT,
    )(*parts)


def solution(mesh):
    in_specs = (
        P(None, "seq", "tp"),
        P(None, "seq", "tp"),
        P(None, "seq", "tp"),
        P(),
        P("tp", None),
    )
    return jax.shard_map(body, mesh=mesh, in_specs=in_specs, out_specs=P(None, "seq", None), check_vma=False)
```

```python
import functools
import math

import jax
import jax.numpy as jnp
from jax import lax
from jax.experimental import pallas as pl
from jax.experimental.pallas import tpu as pltpu
from jax.sharding import PartitionSpec as P

NZ, NX, NY, NH, NC = 8, 2, 4, 2, 2
AXES = ("seq", "tp")
MASKED = -1e30
COLUMNS_BACK = (0, 1, 3, 2)
GROUP = 4
PIECES = 1
LONG = pl.CostEstimate(flops=16 << 30, bytes_accessed=16 << 20, transcendentals=4 << 20)
LIMIT = pltpu.CompilerParams(vmem_limit_bytes=24 * 1024 * 1024)
VMEM = pl.BlockSpec(memory_space=pltpu.VMEM)
HBM = pl.BlockSpec(memory_space=pl.ANY)


def shift(array, move):
    flat = lambda z, x, y, h, c: (((z * NX + x) * NY + y) * NH + h) * NC + c
    devices = [
        (z, x, y, h, c)
        for z in range(NZ) for x in range(NX) for y in range(NY) for h in range(NH) for c in range(NC)
    ]
    return lax.ppermute(array, AXES, [(flat(*d), flat(*move(*d))) for d in devices])


def swap_x(array):
    return shift(array, lambda z, x, y, h, c: (z, 1 - x, y, h, c))


def swap_core(array):
    return shift(array, lambda z, x, y, h, c: (z, x, y, h, 1 - c))


def swap_high(array):
    return shift(array, lambda z, x, y, h, c: (z, x, y, 1 - h, c))


def swap_both(array):
    return shift(array, lambda z, x, y, h, c: (z, 1 - x, y, 1 - h, c))


def shift_z(array, by):
    return shift(array, lambda z, x, y, h, c: ((z + by) % NZ, x, y, h, c))


def shift_y(array, by):
    return shift(array, lambda z, x, y, h, c: (z, x, (y + by) % NY, h, c))


def coordinates():
    seq, tp = lax.axis_index("seq"), lax.axis_index("tp")
    return seq // (NX * NY), (seq // NY) % NX, seq % NY, tp // NC, tp % NC


def row_positions(which, block):
    z, x, y, _, _ = coordinates()
    base = (z * NX + (1 - x if which else x)) * (NY * block) + y * block
    return base + lax.broadcasted_iota(jnp.int32, (block, 1), 0)


def bias_of(first_ref, which, far, block):
    z, _, y, _, _ = coordinates()
    first, last = first_ref[which, :, :1], row_positions(which, block)
    parts = []
    for back in COLUMNS_BACK:
        column = lax.rem(y + NY - back, NY)
        start = lambda layer, x: ((z - layer) * NX + x) * (NY * block) + column * block
        if far:
            shared = start(4, 0) if back == 0 else jnp.where(y >= back, start(0, 1), start(4, 0))
            starts = [shared, start(4, 1), start(3, 0), start(3, 1)]
        else:
            starts = [start(0, 0)] + ([start(0, 1)] if back == 0 else [])
            starts += [start(layer, x) for layer in (1, 2) for x in (0, 1)]
        tiles = []
        for i in range(0, len(starts), 2):
            pair = starts[i:i + 2]
            lane = lax.broadcasted_iota(jnp.int32, (1, len(pair) * block), 1)
            at = pair[0] + lane if len(pair) == 1 else jnp.where(lane < block, pair[0] + lane, pair[1] + lane - block)
            tiles.append(jnp.where((at >= first) & (at <= last), 0.0, MASKED))
        parts.append(jnp.concatenate(tiles, axis=1))
    return parts


def attend_group(queries, kv_refs, bias, top, scale):
    size = queries.shape[1]
    scores = []
    for ref, part in zip(kv_refs, bias):
        keys = ref[0].reshape(-1, size)
        raw = lax.dot_general(queries, keys, (((1,), (1,)), ((), ())), preferred_element_type=jnp.float32)
        scores.append((raw.reshape(GROUP, -1, raw.shape[1]) + part[None]).reshape(raw.shape))
    highest = functools.reduce(jnp.maximum, [jnp.max(s, axis=1, keepdims=True) for s in scores])
    if top is not None:
        highest = jnp.maximum(highest, top)
    offset = highest * scale
    total, mixed = 0.0, 0.0
    for ref, s in zip(kv_refs, scores):
        kept = jnp.exp2(s * scale - offset)
        total = total + jnp.sum(kept, axis=1, keepdims=True)
        mixed = mixed + jnp.dot(kept.astype(jnp.bfloat16), ref[1].reshape(-1, size), preferred_element_type=jnp.float32)
    return highest, total, mixed


def near_kernel(heads, size, block, first_ref, own_ref, other_ref, k0, k1, k2, k3, mixed_ref, stat_ref):
    scale = math.log2(math.e) / math.sqrt(size)
    lane = lax.broadcasted_iota(jnp.int32, (block, 128), 1)
    for which, query_ref in enumerate((own_ref, other_ref)):
        bias = bias_of(first_ref, which, False, block)
        stats = jnp.zeros((block, 128), jnp.float32)
        for start in range(0, heads, GROUP):
            group = range(start, start + GROUP)
            queries = jnp.concatenate([query_ref[:, h * size:(h + 1) * size] for h in group], axis=0)
            highest, total, mixed = attend_group(queries, (k0, k1, k2, k3), bias, None, scale)
            for i, head in enumerate(group):
                part = slice(i * block, (i + 1) * block)
                mixed_ref[which, :, head * size:(head + 1) * size] = mixed[part]
                stats = jnp.where(lane == head, highest[part], stats)
                stats = jnp.where(lane == heads + head, total[part], stats)
        stat_ref[which] = stats


def far_block(heads, size, block, which, first_ref, query_ref, kv_refs, mixed_ref, stat_ref, context_ref):
    scale = math.log2(math.e) / math.sqrt(size)
    bias = bias_of(first_ref, which, True, block)
    stats = stat_ref[which]
    for start in range(0, heads, GROUP):
        group = range(start, start + GROUP)
        queries = jnp.concatenate([query_ref[:, h * size:(h + 1) * size] for h in group], axis=0)
        old_top = jnp.concatenate([stats[:, h:h + 1] for h in group], axis=0)
        highest, total, mixed = attend_group(queries, kv_refs, bias, old_top, scale)
        fade = jnp.exp2((old_top - highest) * scale)
        for i, head in enumerate(group):
            part, at = slice(i * block, (i + 1) * block), slice(head * size, (head + 1) * size)
            whole = total[part] + stats[:, heads + head:heads + head + 1] * fade[part]
            context_ref[:, at] = ((mixed[part] + mixed_ref[which, :, at] * fade[part]) / whole).astype(jnp.bfloat16)


def far_kernel(heads, size, block, first_ref, query_ref, k0, k1, k2, k3, mixed_ref, stat_ref, context_ref):
    far_block(heads, size, block, 1, first_ref, query_ref, (k0, k1, k2, k3), mixed_ref, stat_ref, context_ref)


def pack_kernel(block, unit_ref, third_ref, fourth_ref, *out_refs):
    y = coordinates()[2]
    for by, out_ref in zip(COLUMNS_BACK, out_refs):
        shared = fourth_ref[:, :block]
        if by:
            shared = jnp.where(y + by < NY, unit_ref[:, block:], shared)
        out_ref[:, :block] = shared
        out_ref[:, block:2 * block] = fourth_ref[:, block:]
        out_ref[:, 2 * block:] = third_ref[...]


def project(own_half, context_ref, weight_ref, out_ref, pieces=1, piece=0):
    width = out_ref.shape[1]
    core = coordinates()[-1]
    which = core if own_half else 1 - core
    columns = pl.ds(pl.multiple_of((which * pieces + piece) * width, width), width)
    out_ref[...] = jnp.dot(context_ref[...], weight_ref[:, columns], preferred_element_type=jnp.float32).astype(out_ref.dtype)


def project_kernel(own_half, context_ref, weight_ref, out_ref):
    project(own_half, context_ref, weight_ref, out_ref)


def far_project_kernel(heads, size, block, first_ref, query_ref, k0, k1, k2, k3, mixed_ref, stat_ref, weight_ref, give0_ref, give1_ref, keep_ref, context_ref):
    far_block(heads, size, block, 0, first_ref, query_ref, (k0, k1, k2, k3), mixed_ref, stat_ref, context_ref)
    project(False, context_ref, weight_ref, give0_ref, 2, 0)
    project(False, context_ref, weight_ref, give1_ref, 2, 1)
    project(True, context_ref, weight_ref, keep_ref)


def place_kernel(pieces, *refs):
    parts, out_ref, sems = refs[:4 * pieces], refs[-2], refs[-1]
    _, x, _, high, core = coordinates()
    batch = x ^ high
    width = parts[0].shape[1]
    copies = []
    for i, part in enumerate(parts):
        row = 1 - batch if (i // pieces) % 2 else batch
        half = 1 - core if i // pieces >= 2 else core
        at = pl.multiple_of(half * (pieces * width) + (i % pieces) * width, 128)
        copies.append(pltpu.make_async_copy(part, out_ref.at[row, :, pl.ds(at, width)], sems.at[i]))
    for copy in copies:
        copy.start()
    for copy in copies:
        copy.wait()


def body(queries, key_projected, values, segments, out_weight):
    batches, block, width = queries.shape
    size = key_projected.shape[2]
    heads = width // size
    features = out_weight.shape[1]
    z, x, y, high, core = coordinates()
    batch = x ^ high
    pick = lambda a, i: lax.dynamic_index_in_dim(a, i, 0, keepdims=False)

    pair = jnp.stack([key_projected, values], axis=1)
    mine, theirs = lax.optimization_barrier((pick(pair, batch), pick(pair, 1 - batch)))
    theirs = swap_x(theirs)
    unit = jnp.concatenate([jnp.where(x == 0, mine, theirs), jnp.where(x == 0, theirs, mine)], axis=1)
    back = [unit] + [shift_z(unit, by) for by in (1, 2, 3, 4)]
    near = jnp.concatenate(back[:3], axis=1)
    near_sent = jnp.concatenate([back[0][:, :block], back[1], back[2]], axis=1)
    near_all = [near] + [shift_y(near_sent, by) for by in COLUMNS_BACK[1:]]
    packed = pl.pallas_call(
        functools.partial(pack_kernel, block),
        out_shape=[jax.ShapeDtypeStruct((2, 4 * block, size), jnp.bfloat16)] * NY,
        in_specs=[VMEM] * 3,
        out_specs=[VMEM] * NY,
        compiler_params=LIMIT,
    )(back[0], back[3], back[4])
    far_all = [packed[0]] + [shift_y(array, by) for array, by in zip(packed[1:], COLUMNS_BACK[1:])]
    own_q = pick(queries, batch)
    other_q = swap_x(pick(queries, 1 - batch))

    seg = pick(segments, batch)
    starts = jnp.sum((seg[None, :] < jnp.arange(4, dtype=jnp.int32)[:, None]).astype(jnp.int32), axis=1)
    positions = jnp.stack([row_positions(which, block) for which in (0, 1)])
    first = jnp.max(jnp.where(starts <= positions, starts, 0), axis=2, keepdims=True)
    first = jnp.broadcast_to(first, (2, block, 128))

    mixed, stats = pl.pallas_call(
        functools.partial(near_kernel, heads, size, block),
        out_shape=(
            jax.ShapeDtypeStruct((2, block, width), jnp.float32),
            jax.ShapeDtypeStruct((2, block, 128), jnp.float32),
        ),
        in_specs=[VMEM] * 7,
        out_specs=(VMEM, VMEM),
        compiler_params=LIMIT,
        cost_estimate=LONG,
    )(first, own_q, other_q, *near_all)

    other_context = pl.pallas_call(
        functools.partial(far_kernel, heads, size, block),
        out_shape=jax.ShapeDtypeStruct((block, width), jnp.bfloat16),
        in_specs=[VMEM] * 8,
        out_specs=VMEM,
        compiler_params=LIMIT,
    )(first, other_q, *far_all, mixed, stats)

    def projected(own_half, dtype):
        return pl.pallas_call(
            functools.partial(project_kernel, own_half),
            out_shape=jax.ShapeDtypeStruct((block, features // 2), dtype),
            in_specs=[VMEM, VMEM],
            out_specs=VMEM,
            compiler_params=LIMIT,
        )(other_context, out_weight)

    def cut(array):
        return jnp.split(array, PIECES, axis=1)

    given = swap_core(projected(False, jnp.bfloat16))
    sent = (projected(True, jnp.float32) + given.astype(jnp.float32)).astype(jnp.bfloat16)
    sent, own_q = lax.optimization_barrier((sent, own_q))
    arrived = [swap_both(piece) for piece in cut(sent)]
    given0, given1, kept = pl.pallas_call(
        functools.partial(far_project_kernel, heads, size, block),
        out_shape=(
            jax.ShapeDtypeStruct((block, features // 4), jnp.bfloat16),
            jax.ShapeDtypeStruct((block, features // 4), jnp.bfloat16),
            jax.ShapeDtypeStruct((block, features // 2), jnp.float32),
        ),
        in_specs=[VMEM] * 9,
        out_specs=(VMEM, VMEM, VMEM),
        scratch_shapes=[pltpu.VMEM((block, width), jnp.bfloat16)],
        compiler_params=LIMIT,
    )(first, own_q, *far_all, mixed, stats, out_weight)
    given = jnp.concatenate([swap_core(given0), swap_core(given1)], axis=1)
    summed = kept + given.astype(jnp.float32)

    final = [(s + a.astype(jnp.float32)).astype(jnp.bfloat16) for s, a in zip(cut(summed), arrived)]
    other = [swap_high(f) for f in final]

    parts = final + other + [swap_core(f) for f in final] + [swap_core(o) for o in other]
    return pl.pallas_call(
        functools.partial(place_kernel, PIECES),
        out_shape=jax.ShapeDtypeStruct((batches, block, features), jnp.bfloat16),
        in_specs=[VMEM] * len(parts),
        out_specs=HBM,
        scratch_shapes=[pltpu.SemaphoreType.DMA((len(parts),))],
        compiler_params=LIMIT,
    )(*parts)


def solution(mesh):
    in_specs = (
        P(None, "seq", "tp"),
        P(None, "seq", "tp"),
        P(None, "seq", "tp"),
        P(),
        P("tp", None),
    )
    return jax.shard_map(body, mesh=mesh, in_specs=in_specs, out_specs=P(None, "seq", None), check_vma=False)
```

```python
import functools
import math

import jax
import jax.numpy as jnp
from jax import lax
from jax.experimental import pallas as pl
from jax.experimental.pallas import tpu as pltpu
from jax.sharding import PartitionSpec as P

NZ, NX, NY, NH, NC = 8, 2, 4, 2, 2
AXES = ("seq", "tp")
MASKED = -1e30
COLUMNS_BACK = (0, 1, 3, 2)
GROUP = 4
PIECES = 1
LONG = pl.CostEstimate(flops=16 << 30, bytes_accessed=16 << 20, transcendentals=4 << 20)
LIMIT = pltpu.CompilerParams(vmem_limit_bytes=24 * 1024 * 1024)
VMEM = pl.BlockSpec(memory_space=pltpu.VMEM)
HBM = pl.BlockSpec(memory_space=pl.ANY)


def shift(array, move):
    flat = lambda z, x, y, h, c: (((z * NX + x) * NY + y) * NH + h) * NC + c
    devices = [
        (z, x, y, h, c)
        for z in range(NZ) for x in range(NX) for y in range(NY) for h in range(NH) for c in range(NC)
    ]
    return lax.ppermute(array, AXES, [(flat(*d), flat(*move(*d))) for d in devices])


def swap_x(array):
    return shift(array, lambda z, x, y, h, c: (z, 1 - x, y, h, c))


def swap_core(array):
    return shift(array, lambda z, x, y, h, c: (z, x, y, h, 1 - c))


def swap_high(array):
    return shift(array, lambda z, x, y, h, c: (z, x, y, 1 - h, c))


def swap_both(array):
    return shift(array, lambda z, x, y, h, c: (z, 1 - x, y, 1 - h, c))


def shift_z(array, by):
    return shift(array, lambda z, x, y, h, c: ((z + by) % NZ, x, y, h, c))


def shift_y(array, by):
    return shift(array, lambda z, x, y, h, c: (z, x, (y + by) % NY, h, c))


def coordinates():
    seq, tp = lax.axis_index("seq"), lax.axis_index("tp")
    return seq // (NX * NY), (seq // NY) % NX, seq % NY, tp // NC, tp % NC


def row_positions(which, block):
    z, x, y, _, _ = coordinates()
    base = (z * NX + (1 - x if which else x)) * (NY * block) + y * block
    return base + lax.broadcasted_iota(jnp.int32, (block, 1), 0)


def bias_of(first_ref, which, far, block):
    z, _, y, _, _ = coordinates()
    first, last = first_ref[which, :, :1], row_positions(which, block)
    parts = []
    for back in COLUMNS_BACK:
        column = lax.rem(y + NY - back, NY)
        start = lambda layer, x: ((z - layer) * NX + x) * (NY * block) + column * block
        if far:
            shared = start(4, 0) if back == 0 else jnp.where(y >= back, start(0, 1), start(4, 0))
            starts = [shared, start(4, 1), start(3, 0), start(3, 1)]
        else:
            starts = [start(0, 0)] + ([start(0, 1)] if back == 0 else [])
            starts += [start(layer, x) for layer in (1, 2) for x in (0, 1)]
        tiles = []
        for i in range(0, len(starts), 2):
            pair = starts[i:i + 2]
            lane = lax.broadcasted_iota(jnp.int32, (1, len(pair) * block), 1)
            at = pair[0] + lane if len(pair) == 1 else jnp.where(lane < block, pair[0] + lane, pair[1] + lane - block)
            tiles.append(jnp.where((at >= first) & (at <= last), 0.0, MASKED))
        parts.append(jnp.concatenate(tiles, axis=1))
    return parts


def attend_group(queries, kv_refs, bias, top, scale):
    size = queries.shape[1]
    scores = []
    for ref, part in zip(kv_refs, bias):
        keys = ref[0].reshape(-1, size)
        raw = lax.dot_general(queries, keys, (((1,), (1,)), ((), ())), preferred_element_type=jnp.float32)
        scores.append((raw.reshape(GROUP, -1, raw.shape[1]) + part[None]).reshape(raw.shape))
    highest = functools.reduce(jnp.maximum, [jnp.max(s, axis=1, keepdims=True) for s in scores])
    if top is not None:
        highest = jnp.maximum(highest, top)
    offset = highest * scale
    total, mixed = 0.0, 0.0
    for ref, s in zip(kv_refs, scores):
        kept = jnp.exp2(s * scale - offset)
        total = total + jnp.sum(kept, axis=1, keepdims=True)
        mixed = mixed + jnp.dot(kept.astype(jnp.bfloat16), ref[1].reshape(-1, size), preferred_element_type=jnp.float32)
    return highest, total, mixed


def near_kernel(heads, size, block, first_ref, own_ref, other_ref, k0, k1, k2, k3, far_own, mixed_ref, stat_ref):
    scale = math.log2(math.e) / math.sqrt(size)
    lane = lax.broadcasted_iota(jnp.int32, (block, 128), 1)
    for which, query_ref in enumerate((own_ref, other_ref)):
        bias = bias_of(first_ref, which, False, block) + bias_of(first_ref, which, True, block)[:1]
        stats = jnp.zeros((block, 128), jnp.float32)
        for start in range(0, heads, GROUP):
            group = range(start, start + GROUP)
            queries = jnp.concatenate([query_ref[:, h * size:(h + 1) * size] for h in group], axis=0)
            highest, total, mixed = attend_group(queries, (k0, k1, k2, k3, far_own), bias, None, scale)
            for i, head in enumerate(group):
                part = slice(i * block, (i + 1) * block)
                mixed_ref[which, :, head * size:(head + 1) * size] = mixed[part]
                stats = jnp.where(lane == head, highest[part], stats)
                stats = jnp.where(lane == heads + head, total[part], stats)
        stat_ref[which] = stats


def far_block(heads, size, block, which, first_ref, query_ref, kv_refs, mixed_ref, stat_ref, context_ref):
    scale = math.log2(math.e) / math.sqrt(size)
    bias = bias_of(first_ref, which, True, block)[1:]
    stats = stat_ref[which]
    for start in range(0, heads, GROUP):
        group = range(start, start + GROUP)
        queries = jnp.concatenate([query_ref[:, h * size:(h + 1) * size] for h in group], axis=0)
        old_top = jnp.concatenate([stats[:, h:h + 1] for h in group], axis=0)
        highest, total, mixed = attend_group(queries, kv_refs, bias, old_top, scale)
        fade = jnp.exp2((old_top - highest) * scale)
        for i, head in enumerate(group):
            part, at = slice(i * block, (i + 1) * block), slice(head * size, (head + 1) * size)
            whole = total[part] + stats[:, heads + head:heads + head + 1] * fade[part]
            context_ref[:, at] = ((mixed[part] + mixed_ref[which, :, at] * fade[part]) / whole).astype(jnp.bfloat16)


def far_kernel(heads, size, block, first_ref, query_ref, k1, k2, k3, mixed_ref, stat_ref, context_ref):
    far_block(heads, size, block, 1, first_ref, query_ref, (k1, k2, k3), mixed_ref, stat_ref, context_ref)


def pack_kernel(block, unit_ref, third_ref, fourth_ref, *out_refs):
    y = coordinates()[2]
    for by, out_ref in zip(COLUMNS_BACK, out_refs):
        shared = fourth_ref[:, :block]
        if by:
            shared = jnp.where(y + by < NY, unit_ref[:, block:], shared)
        out_ref[:, :block] = shared
        out_ref[:, block:2 * block] = fourth_ref[:, block:]
        out_ref[:, 2 * block:] = third_ref[...]


def project(own_half, context_ref, weight_ref, out_ref, pieces=1, piece=0):
    width = out_ref.shape[1]
    core = coordinates()[-1]
    which = core if own_half else 1 - core
    columns = pl.ds(pl.multiple_of((which * pieces + piece) * width, width), width)
    out_ref[...] = jnp.dot(context_ref[...], weight_ref[:, columns], preferred_element_type=jnp.float32).astype(out_ref.dtype)


def project_kernel(own_half, context_ref, weight_ref, out_ref):
    project(own_half, context_ref, weight_ref, out_ref)


def far_project_kernel(heads, size, block, first_ref, query_ref, k1, k2, k3, mixed_ref, stat_ref, weight_ref, give0_ref, give1_ref, keep_ref, context_ref):
    far_block(heads, size, block, 0, first_ref, query_ref, (k1, k2, k3), mixed_ref, stat_ref, context_ref)
    project(False, context_ref, weight_ref, give0_ref, 2, 0)
    project(False, context_ref, weight_ref, give1_ref, 2, 1)
    project(True, context_ref, weight_ref, keep_ref)


def place_kernel(pieces, *refs):
    parts, out_ref, sems = refs[:4 * pieces], refs[-2], refs[-1]
    _, x, _, high, core = coordinates()
    batch = x ^ high
    width = parts[0].shape[1]
    copies = []
    for i, part in enumerate(parts):
        row = 1 - batch if (i // pieces) % 2 else batch
        half = 1 - core if i // pieces >= 2 else core
        at = pl.multiple_of(half * (pieces * width) + (i % pieces) * width, 128)
        copies.append(pltpu.make_async_copy(part, out_ref.at[row, :, pl.ds(at, width)], sems.at[i]))
    for copy in copies:
        copy.start()
    for copy in copies:
        copy.wait()


def body(queries, key_projected, values, segments, out_weight):
    batches, block, width = queries.shape
    size = key_projected.shape[2]
    heads = width // size
    features = out_weight.shape[1]
    z, x, y, high, core = coordinates()
    batch = x ^ high
    pick = lambda a, i: lax.dynamic_index_in_dim(a, i, 0, keepdims=False)

    pair = jnp.stack([key_projected, values], axis=1)
    mine, theirs = lax.optimization_barrier((pick(pair, batch), pick(pair, 1 - batch)))
    theirs = swap_x(theirs)
    unit = jnp.concatenate([jnp.where(x == 0, mine, theirs), jnp.where(x == 0, theirs, mine)], axis=1)
    back = [unit] + [shift_z(unit, by) for by in (1, 2, 3, 4)]
    near = jnp.concatenate(back[:3], axis=1)
    near_sent = jnp.concatenate([back[0][:, :block], back[1], back[2]], axis=1)
    near_all = [near] + [shift_y(near_sent, by) for by in COLUMNS_BACK[1:]]
    packed = pl.pallas_call(
        functools.partial(pack_kernel, block),
        out_shape=[jax.ShapeDtypeStruct((2, 4 * block, size), jnp.bfloat16)] * NY,
        in_specs=[VMEM] * 3,
        out_specs=[VMEM] * NY,
        compiler_params=LIMIT,
    )(back[0], back[3], back[4])
    far_all = [packed[0]] + [shift_y(array, by) for array, by in zip(packed[1:], COLUMNS_BACK[1:])]
    own_q = pick(queries, batch)
    other_q = swap_x(pick(queries, 1 - batch))

    seg = pick(segments, batch)
    starts = jnp.sum((seg[None, :] < jnp.arange(4, dtype=jnp.int32)[:, None]).astype(jnp.int32), axis=1)
    positions = jnp.stack([row_positions(which, block) for which in (0, 1)])
    first = jnp.max(jnp.where(starts <= positions, starts, 0), axis=2, keepdims=True)
    first = jnp.broadcast_to(first, (2, block, 128))

    mixed, stats = pl.pallas_call(
        functools.partial(near_kernel, heads, size, block),
        out_shape=(
            jax.ShapeDtypeStruct((2, block, width), jnp.float32),
            jax.ShapeDtypeStruct((2, block, 128), jnp.float32),
        ),
        in_specs=[VMEM] * 8,
        out_specs=(VMEM, VMEM),
        compiler_params=LIMIT,
        cost_estimate=LONG,
    )(first, own_q, other_q, *near_all, far_all[0])

    other_context = pl.pallas_call(
        functools.partial(far_kernel, heads, size, block),
        out_shape=jax.ShapeDtypeStruct((block, width), jnp.bfloat16),
        in_specs=[VMEM] * 7,
        out_specs=VMEM,
        compiler_params=LIMIT,
    )(first, other_q, *far_all[1:], mixed, stats)

    def projected(own_half, dtype):
        return pl.pallas_call(
            functools.partial(project_kernel, own_half),
            out_shape=jax.ShapeDtypeStruct((block, features // 2), dtype),
            in_specs=[VMEM, VMEM],
            out_specs=VMEM,
            compiler_params=LIMIT,
        )(other_context, out_weight)

    def cut(array):
        return jnp.split(array, PIECES, axis=1)

    given = swap_core(projected(False, jnp.bfloat16))
    sent = (projected(True, jnp.float32) + given.astype(jnp.float32)).astype(jnp.bfloat16)
    sent, own_q = lax.optimization_barrier((sent, own_q))
    arrived = [swap_both(piece) for piece in cut(sent)]
    given0, given1, kept = pl.pallas_call(
        functools.partial(far_project_kernel, heads, size, block),
        out_shape=(
            jax.ShapeDtypeStruct((block, features // 4), jnp.bfloat16),
            jax.ShapeDtypeStruct((block, features // 4), jnp.bfloat16),
            jax.ShapeDtypeStruct((block, features // 2), jnp.float32),
        ),
        in_specs=[VMEM] * 8,
        out_specs=(VMEM, VMEM, VMEM),
        scratch_shapes=[pltpu.VMEM((block, width), jnp.bfloat16)],
        compiler_params=LIMIT,
    )(first, own_q, *far_all[1:], mixed, stats, out_weight)
    given = jnp.concatenate([swap_core(given0), swap_core(given1)], axis=1)
    summed = kept + given.astype(jnp.float32)

    final = [(s + a.astype(jnp.float32)).astype(jnp.bfloat16) for s, a in zip(cut(summed), arrived)]
    other = [swap_high(f) for f in final]

    parts = final + other + [swap_core(f) for f in final] + [swap_core(o) for o in other]
    return pl.pallas_call(
        functools.partial(place_kernel, PIECES),
        out_shape=jax.ShapeDtypeStruct((batches, block, features), jnp.bfloat16),
        in_specs=[VMEM] * len(parts),
        out_specs=HBM,
        scratch_shapes=[pltpu.SemaphoreType.DMA((len(parts),))],
        compiler_params=LIMIT,
    )(*parts)


def solution(mesh):
    in_specs = (
        P(None, "seq", "tp"),
        P(None, "seq", "tp"),
        P(None, "seq", "tp"),
        P(),
        P("tp", None),
    )
    return jax.shard_map(body, mesh=mesh, in_specs=in_specs, out_specs=P(None, "seq", None), check_vma=False)
```

```python
import functools
import math

import jax
import jax.numpy as jnp
from jax import lax
from jax.experimental import pallas as pl
from jax.experimental.pallas import tpu as pltpu
from jax.sharding import PartitionSpec as P

NZ, NX, NY, NH, NC = 8, 2, 4, 2, 2
AXES = ("seq", "tp")
MASKED = -1e30
COLUMNS_BACK = (0, 1, 3, 2)
GROUP = 4
PIECES = 1
LONG = pl.CostEstimate(flops=16 << 30, bytes_accessed=16 << 20, transcendentals=4 << 20)
LIMIT = pltpu.CompilerParams(vmem_limit_bytes=24 * 1024 * 1024)
VMEM = pl.BlockSpec(memory_space=pltpu.VMEM)
HBM = pl.BlockSpec(memory_space=pl.ANY)


def shift(array, move):
    flat = lambda z, x, y, h, c: (((z * NX + x) * NY + y) * NH + h) * NC + c
    devices = [
        (z, x, y, h, c)
        for z in range(NZ) for x in range(NX) for y in range(NY) for h in range(NH) for c in range(NC)
    ]
    return lax.ppermute(array, AXES, [(flat(*d), flat(*move(*d))) for d in devices])


def swap_x(array):
    return shift(array, lambda z, x, y, h, c: (z, 1 - x, y, h, c))


def swap_core(array):
    return shift(array, lambda z, x, y, h, c: (z, x, y, h, 1 - c))


def swap_high(array):
    return shift(array, lambda z, x, y, h, c: (z, x, y, 1 - h, c))


def swap_both(array):
    return shift(array, lambda z, x, y, h, c: (z, 1 - x, y, 1 - h, c))


def shift_z(array, by):
    return shift(array, lambda z, x, y, h, c: ((z + by) % NZ, x, y, h, c))


def shift_y(array, by):
    return shift(array, lambda z, x, y, h, c: (z, x, (y + by) % NY, h, c))


def coordinates():
    seq, tp = lax.axis_index("seq"), lax.axis_index("tp")
    return seq // (NX * NY), (seq // NY) % NX, seq % NY, tp // NC, tp % NC


def row_positions(which, block):
    z, x, y, _, _ = coordinates()
    base = (z * NX + (1 - x if which else x)) * (NY * block) + y * block
    return base + lax.broadcasted_iota(jnp.int32, (block, 1), 0)


def bias_of(first_ref, which, far, block):
    z, _, y, _, _ = coordinates()
    first, last = first_ref[which, :, :1], row_positions(which, block)
    parts = []
    for back in COLUMNS_BACK:
        column = lax.rem(y + NY - back, NY)
        start = lambda layer, x: ((z - layer) * NX + x) * (NY * block) + column * block
        if far:
            shared = start(4, 0) if back == 0 else jnp.where(y >= back, start(0, 1), start(4, 0))
            starts = [shared, start(4, 1), start(3, 0), start(3, 1)]
        else:
            starts = [start(0, 0)] + ([start(0, 1)] if back == 0 else [])
            starts += [start(layer, x) for layer in (1, 2) for x in (0, 1)]
        tiles = []
        for i in range(0, len(starts), 2):
            pair = starts[i:i + 2]
            lane = lax.broadcasted_iota(jnp.int32, (1, len(pair) * block), 1)
            at = pair[0] + lane if len(pair) == 1 else jnp.where(lane < block, pair[0] + lane, pair[1] + lane - block)
            tiles.append(jnp.where((at >= first) & (at <= last), 0.0, MASKED))
        parts.append(jnp.concatenate(tiles, axis=1))
    return parts


def attend_group(queries, kv_refs, bias, top, scale):
    size = queries.shape[1]
    scores = []
    for ref, part in zip(kv_refs, bias):
        keys = ref[0].reshape(-1, size)
        raw = lax.dot_general(queries, keys, (((1,), (1,)), ((), ())), preferred_element_type=jnp.float32)
        scores.append((raw.reshape(GROUP, -1, raw.shape[1]) + part[None]).reshape(raw.shape))
    highest = functools.reduce(jnp.maximum, [jnp.max(s, axis=1, keepdims=True) for s in scores])
    if top is not None:
        highest = jnp.maximum(highest, top)
    offset = highest * scale
    total, mixed = 0.0, 0.0
    for ref, s in zip(kv_refs, scores):
        kept = jnp.exp2(s * scale - offset)
        total = total + jnp.sum(kept, axis=1, keepdims=True)
        mixed = mixed + jnp.dot(kept.astype(jnp.bfloat16), ref[1].reshape(-1, size), preferred_element_type=jnp.float32)
    return highest, total, mixed


def near_kernel(heads, size, block, first_ref, own_ref, other_ref, k0, k1, k2, k3, far_own, mixed_ref, stat_ref):
    scale = math.log2(math.e) / math.sqrt(size)
    lane = lax.broadcasted_iota(jnp.int32, (block, 128), 1)
    for which, query_ref in enumerate((own_ref, other_ref)):
        bias = bias_of(first_ref, which, False, block) + bias_of(first_ref, which, True, block)[:1]
        stats = jnp.zeros((block, 128), jnp.float32)
        for start in range(0, heads, GROUP):
            group = range(start, start + GROUP)
            queries = jnp.concatenate([query_ref[:, h * size:(h + 1) * size] for h in group], axis=0)
            highest, total, mixed = attend_group(queries, (k0, k1, k2, k3, far_own), bias, None, scale)
            for i, head in enumerate(group):
                part = slice(i * block, (i + 1) * block)
                mixed_ref[which, :, head * size:(head + 1) * size] = mixed[part]
                stats = jnp.where(lane == head, highest[part], stats)
                stats = jnp.where(lane == heads + head, total[part], stats)
        stat_ref[which] = stats


def far_block(heads, size, block, which, first_ref, query_ref, kv_refs, mixed_ref, stat_ref, context_ref):
    scale = math.log2(math.e) / math.sqrt(size)
    bias = bias_of(first_ref, which, True, block)[1:]
    stats = stat_ref[which]
    for start in range(0, heads, GROUP):
        group = range(start, start + GROUP)
        queries = jnp.concatenate([query_ref[:, h * size:(h + 1) * size] for h in group], axis=0)
        old_top = jnp.concatenate([stats[:, h:h + 1] for h in group], axis=0)
        highest, total, mixed = attend_group(queries, kv_refs, bias, old_top, scale)
        fade = jnp.exp2((old_top - highest) * scale)
        for i, head in enumerate(group):
            part, at = slice(i * block, (i + 1) * block), slice(head * size, (head + 1) * size)
            whole = total[part] + stats[:, heads + head:heads + head + 1] * fade[part]
            context_ref[:, at] = ((mixed[part] + mixed_ref[which, :, at] * fade[part]) / whole).astype(jnp.bfloat16)


def far_kernel(heads, size, block, first_ref, query_ref, k1, k2, k3, mixed_ref, stat_ref, context_ref):
    far_block(heads, size, block, 1, first_ref, query_ref, (k1, k2, k3), mixed_ref, stat_ref, context_ref)


def pack_kernel(block, unit_ref, third_ref, fourth_ref, *out_refs):
    y = coordinates()[2]
    for by, out_ref in zip(COLUMNS_BACK, out_refs):
        shared = fourth_ref[:, :block]
        if by:
            shared = jnp.where(y + by < NY, unit_ref[:, block:], shared)
        out_ref[:, :block] = shared
        out_ref[:, block:2 * block] = fourth_ref[:, block:]
        out_ref[:, 2 * block:] = third_ref[...]


def project(own_half, context_ref, weight_ref, out_ref, pieces=1, piece=0):
    width = out_ref.shape[1]
    core = coordinates()[-1]
    which = core if own_half else 1 - core
    columns = pl.ds(pl.multiple_of((which * pieces + piece) * width, width), width)
    out_ref[...] = jnp.dot(context_ref[...], weight_ref[:, columns], preferred_element_type=jnp.float32).astype(out_ref.dtype)


def project_kernel(own_half, context_ref, weight_ref, out_ref):
    project(own_half, context_ref, weight_ref, out_ref)


def far_project_kernel(heads, size, block, first_ref, query_ref, k1, k2, k3, mixed_ref, stat_ref, weight_ref, give0_ref, give1_ref, keep_ref, context_ref):
    far_block(heads, size, block, 0, first_ref, query_ref, (k1, k2, k3), mixed_ref, stat_ref, context_ref)
    project(False, context_ref, weight_ref, give0_ref, 2, 0)
    project(False, context_ref, weight_ref, give1_ref, 2, 1)
    project(True, context_ref, weight_ref, keep_ref)


def place_kernel(pieces, *refs):
    parts, out_ref, sems = refs[:4 * pieces], refs[-2], refs[-1]
    _, x, _, high, core = coordinates()
    batch = x ^ high
    width = parts[0].shape[1]
    copies = []
    for i, part in enumerate(parts):
        row = 1 - batch if (i // pieces) % 2 else batch
        half = 1 - core if i // pieces >= 2 else core
        at = pl.multiple_of(half * (pieces * width) + (i % pieces) * width, 128)
        copies.append(pltpu.make_async_copy(part, out_ref.at[row, :, pl.ds(at, width)], sems.at[i]))
    for copy in copies:
        copy.start()
    for copy in copies:
        copy.wait()


def body(queries, key_projected, values, segments, out_weight):
    batches, block, width = queries.shape
    size = key_projected.shape[2]
    heads = width // size
    features = out_weight.shape[1]
    z, x, y, high, core = coordinates()
    batch = x ^ high
    pick = lambda a, i: lax.dynamic_index_in_dim(a, i, 0, keepdims=False)

    pair = jnp.stack([key_projected, values], axis=1)
    mine, theirs = lax.optimization_barrier((pick(pair, batch), pick(pair, 1 - batch)))
    theirs = swap_x(theirs)
    unit = jnp.concatenate([jnp.where(x == 0, mine, theirs), jnp.where(x == 0, theirs, mine)], axis=1)
    moved = {by: shift_z(unit, by) for by in (3, 4, 2, 1)}
    back = [unit] + [moved[by] for by in (1, 2, 3, 4)]
    near = jnp.concatenate(back[:3], axis=1)
    near_sent = jnp.concatenate([back[0][:, :block], back[1], back[2]], axis=1)
    near_all = [near] + [shift_y(near_sent, by) for by in COLUMNS_BACK[1:]]
    packed = pl.pallas_call(
        functools.partial(pack_kernel, block),
        out_shape=[jax.ShapeDtypeStruct((2, 4 * block, size), jnp.bfloat16)] * NY,
        in_specs=[VMEM] * 3,
        out_specs=[VMEM] * NY,
        compiler_params=LIMIT,
    )(back[0], back[3], back[4])
    far_all = [packed[0]] + [shift_y(array, by) for array, by in zip(packed[1:], COLUMNS_BACK[1:])]
    own_q = pick(queries, batch)
    other_q = swap_x(pick(queries, 1 - batch))

    seg = pick(segments, batch)
    starts = jnp.sum((seg[None, :] < jnp.arange(4, dtype=jnp.int32)[:, None]).astype(jnp.int32), axis=1)
    positions = jnp.stack([row_positions(which, block) for which in (0, 1)])
    first = jnp.max(jnp.where(starts <= positions, starts, 0), axis=2, keepdims=True)
    first = jnp.broadcast_to(first, (2, block, 128))

    mixed, stats = pl.pallas_call(
        functools.partial(near_kernel, heads, size, block),
        out_shape=(
            jax.ShapeDtypeStruct((2, block, width), jnp.float32),
            jax.ShapeDtypeStruct((2, block, 128), jnp.float32),
        ),
        in_specs=[VMEM] * 8,
        out_specs=(VMEM, VMEM),
        compiler_params=LIMIT,
        cost_estimate=LONG,
    )(first, own_q, other_q, *near_all, far_all[0])

    other_context = pl.pallas_call(
        functools.partial(far_kernel, heads, size, block),
        out_shape=jax.ShapeDtypeStruct((block, width), jnp.bfloat16),
        in_specs=[VMEM] * 7,
        out_specs=VMEM,
        compiler_params=LIMIT,
    )(first, other_q, *far_all[1:], mixed, stats)

    def projected(own_half, dtype):
        return pl.pallas_call(
            functools.partial(project_kernel, own_half),
            out_shape=jax.ShapeDtypeStruct((block, features // 2), dtype),
            in_specs=[VMEM, VMEM],
            out_specs=VMEM,
            compiler_params=LIMIT,
        )(other_context, out_weight)

    def cut(array):
        return jnp.split(array, PIECES, axis=1)

    given = swap_core(projected(False, jnp.bfloat16))
    sent = (projected(True, jnp.float32) + given.astype(jnp.float32)).astype(jnp.bfloat16)
    sent, own_q = lax.optimization_barrier((sent, own_q))
    arrived = [swap_both(piece) for piece in cut(sent)]
    given0, given1, kept = pl.pallas_call(
        functools.partial(far_project_kernel, heads, size, block),
        out_shape=(
            jax.ShapeDtypeStruct((block, features // 4), jnp.bfloat16),
            jax.ShapeDtypeStruct((block, features // 4), jnp.bfloat16),
            jax.ShapeDtypeStruct((block, features // 2), jnp.float32),
        ),
        in_specs=[VMEM] * 8,
        out_specs=(VMEM, VMEM, VMEM),
        scratch_shapes=[pltpu.VMEM((block, width), jnp.bfloat16)],
        compiler_params=LIMIT,
    )(first, own_q, *far_all[1:], mixed, stats, out_weight)
    given = jnp.concatenate([swap_core(given0), swap_core(given1)], axis=1)
    summed = kept + given.astype(jnp.float32)

    final = [(s + a.astype(jnp.float32)).astype(jnp.bfloat16) for s, a in zip(cut(summed), arrived)]
    other = [swap_high(f) for f in final]

    parts = final + other + [swap_core(f) for f in final] + [swap_core(o) for o in other]
    return pl.pallas_call(
        functools.partial(place_kernel, PIECES),
        out_shape=jax.ShapeDtypeStruct((batches, block, features), jnp.bfloat16),
        in_specs=[VMEM] * len(parts),
        out_specs=HBM,
        scratch_shapes=[pltpu.SemaphoreType.DMA((len(parts),))],
        compiler_params=LIMIT,
    )(*parts)


def solution(mesh):
    in_specs = (
        P(None, "seq", "tp"),
        P(None, "seq", "tp"),
        P(None, "seq", "tp"),
        P(),
        P("tp", None),
    )
    return jax.shard_map(body, mesh=mesh, in_specs=in_specs, out_specs=P(None, "seq", None), check_vma=False)
```
